32 devices in a mesh: gx: 8 (over y, x, core), gy: 4 (over z).
Axes of the slice: x: 2, y: 2, z: 4, core: 2. Of those that a mesh axis runs over, the one named last changes fastest.
Arguments:
- source: float32 [1, 32, 128, 512], P(None, None, 'gx', 'gy'), may hold values from -6 to 6
- first_guess: float32 [1, 32, 128, 512], P(None, None, 'gx', 'gy'), may hold values from -6 to 6
- metric: float32 [128, 512], P('gx', 'gy'), may hold values from 0.5 to 2
- terrain_slope: float32 [128, 512], P('gx', 'gy'), may hold values from -6 to 6
- profile_rows: float32 [4, 32, 128], P('gy', None, 'gx'), may hold values from -6 to 6
- profile_map: int32 [4], replicated, may hold values from 0 to 3, each once
Outputs:
- multiplier: float32 [1, 32, 128, 512], P(None, None, 'gx', 'gy')
The draws below stay inside these ranges and needn't reach their ends.
Inputs may be any that keep to these rules, and one draw needn't show every extreme that they name: `profile_map`: every row of the profile table is named exactly once.
All inputs are finite; a program needn't handle non-finite values.
Results may differ from the reference program's by a relative error of at most 0.0001.
Values sent between devices are 32-bit elements; how exact they have to be, the bound alone decides.
A program may use at most 64 MiB of HBM per device.

```python
import math
import jax
import jax.numpy as jnp
from jax import lax

MEM = 1
NZ = 32
CY = 128
LEVELS = 4
COARSE = 6
CYCLES = 3
NX = 128
NY = 512
PROF = 4
N_GY = 4


def level_of(rng, dims, split, low, top_value):
    loudness, own = 1.0, jax.random.fold_in(rng, 6)
    for position, shards_of in split:
        draws = jnp.exp(jax.random.uniform(jax.random.fold_in(own, position), (shards_of,), jnp.float32, low / len(split), top_value / len(split)))
        loudness = loudness * jnp.repeat(draws, dims[position] // shards_of).reshape([-1 if axis == position else 1 for axis in range(len(dims))])
    return loudness


def scatter_about(rng, dims, deviation, limit, shards=(), held_as=jnp.bfloat16):
    array = jax.random.normal(rng, dims, jnp.float32) * deviation
    if len(shards) > 0:
        array = level_of(rng, dims, shards, -0.22, 0.18) * array
    return jnp.clip(array, min=-limit, max=limit).astype(held_as)


def setup_inputs(seed: int = 0) -> dict:
    arg_keys = jax.random.split(jax.random.key(seed), 7)
    return {
        "source": scatter_about(arg_keys[0], (MEM, NZ, NX, NY), 1.0, 6.0, ((2, 8), (3, 4)), jnp.float32),
        "first_guess": scatter_about(arg_keys[1], (MEM, NZ, NX, NY), 1.0, 6.0, ((2, 8), (3, 4)), jnp.float32),
        "metric": jnp.clip(jnp.exp(math.log(2.0) - 1.3862944 * jax.random.uniform(arg_keys[2], (NX, NY), jnp.float32) ** level_of(arg_keys[2], (NX, NY), ((0, 8), (1, 4)), -0.2, 0.2)), 0.5, 2.0),
        "terrain_slope": scatter_about(arg_keys[3], (NX, NY), 1.0, 6.0, ((0, 8), (1, 4)), jnp.float32),
        "profile_rows": scatter_about(arg_keys[4], (PROF, NZ, NX), 1.0, 6.0, ((0, 4), (2, 8)), jnp.float32),
        "profile_map": jax.random.permutation(arg_keys[5], PROF).astype(jnp.int32),
    }


SIGMA = 0.05
WEIGHT = 0.8
VERTICAL = 4.0
ALONG_Y = 1.0


def level_coefficients(grid_level):
    along_x = 0.25 ** grid_level
    along_z = VERTICAL * along_x
    centre = SIGMA + 2.0 * along_x + 2.0 * ALONG_Y + 2.0 * along_z
    return along_x, along_z, centre


def apply_operator(values, metric, grid_level):
    along_x, along_z, centre = level_coefficients(grid_level)
    padded = jnp.pad(values, 1)
    middle = padded[1:-1, 1:-1, 1:-1]
    beside = along_x * (padded[1:-1, 2:, 1:-1] + padded[1:-1, :-2, 1:-1])
    beside = beside + ALONG_Y * (padded[1:-1, 1:-1, 2:] + padded[1:-1, 1:-1, :-2])
    beside = beside + along_z * (padded[2:, 1:-1, 1:-1] + padded[:-2, 1:-1, 1:-1])
    return metric * (centre * middle - beside)


def relax_sweep(values, right_side, metric, grid_level):
    centre = level_coefficients(grid_level)[2]
    applied = apply_operator(values, metric, grid_level)
    return values + WEIGHT * (right_side - applied) / (metric * centre)


def restrict(values):
    depth, width, length = values.shape
    return 0.25 * values.reshape(depth // 2, 2, width // 2, 2, length).sum(axis=(1, 3))


def prolong(values):
    return jnp.repeat(jnp.repeat(values, 2, axis=0), 2, axis=1)


def coarsen_metric(metric):
    width, length = metric.shape
    return 0.5 * metric.reshape(width // 2, 2, length).sum(axis=1)


def vcycle(estimate, right_side, metrics, grid_level):
    if grid_level == LEVELS - 1:
        estimate = jnp.zeros_like(right_side)
        for sweep_index in range(COARSE):
            estimate = relax_sweep(estimate, right_side, metrics[grid_level], grid_level)
        return estimate
    smoothed = relax_sweep(estimate, right_side, metrics[grid_level], grid_level)
    residual = right_side - apply_operator(smoothed, metrics[grid_level], grid_level)
    coarse_side = restrict(residual)
    correction = vcycle(jnp.zeros_like(coarse_side), coarse_side, metrics, grid_level + 1)
    corrected = smoothed + prolong(correction)
    return relax_sweep(corrected, right_side, metrics[grid_level], grid_level)


def reference(source, first_guess, metric, terrain_slope, profile_rows, profile_map):
    metrics = [metric]
    for grid_level in range(1, LEVELS):
        metrics.append(coarsen_metric(metrics[-1]))
    tiles = profile_map.reshape(MEM, N_GY).astype(jnp.int32)

    def one_member(inputs):
        member_source, member_guess, member_rows = inputs
        chosen = jnp.take(profile_rows, member_rows, axis=0)
        spread = jnp.repeat(jnp.moveaxis(chosen, 0, -1), CY, axis=-1)
        right_side = member_source + spread * terrain_slope
        estimate = member_guess
        for cycle_number in range(CYCLES):
            estimate = vcycle(estimate, right_side, metrics, 0)
        return estimate

    return lax.map(one_member, (source, first_guess, tiles))
```

```python
import jax
import jax.numpy as jnp
from jax import lax
from jax.experimental import pallas as pl
from jax.experimental.pallas import tpu as pltpu
from jax.sharding import PartitionSpec as P

CYCLES = 3
SWEEPS = 5
SIGMA = 0.05
WEIGHT = 0.8
REACH = 3
NEAR = tuple((dx, dy) for dx in (-1, 0, 1) for dy in (-1, 0, 1) if (dx, dy) != (0, 0))
FAR = tuple(
    (dx, dy) for dx in range(-REACH, REACH + 1) for dy in (-1, 0, 1) if (dx, dy) != (0, 0)
)
MESH = pl.DeviceIdType.MESH


def coefficients(grid_level):
    kx = 0.25**grid_level
    kz = 4.0 * kx
    return kx, kz, SIGMA + 2.0 * kx + 2.0 + 2.0 * kz


def loop(low, high, body, step=1):
    count = (high - low) // step

    def several(i, carry):
        for part in range(step):
            body(low + i * step + part)
        return carry

    lax.fori_loop(0, count, several, 0)
    for i in range(low + count * step, high):
        body(i)


def make_kernel(n_gx, n_gy):
    def kernel(
        source, guess, metric, slope, profile, table,
        out,
        v0, s0, g0, s1, g1, s2, r0, r1, r2, p1, p2, p3,
        m0, m1, m2, w1, w2, w3, mrx, prx, ytx, yrx, g2tx, g2rx, g3tx, g3rx,
        near_send, near_recv, metric_send, metric_recv,
        g2_send, g2_recv, g3_send, g3_recv, prof_send, prof_recv,
    ):
        gx, gy = lax.axis_index("gx"), lax.axis_index("gy")

        def there(dx, dy):
            x, y = gx + dx, gy + dy
            inside = jnp.logical_and(x >= 0, x < n_gx)
            return jnp.logical_and(inside, jnp.logical_and(y >= 0, y < n_gy))

        def device(dx, dy):
            return (gx + dx, gy + dy)

        lane = lax.broadcasted_iota(jnp.int32, (1, 128), 1)
        plus = jnp.where(gy + 1 < n_gy, 1.0, 0.0).astype(jnp.float32)
        minus = jnp.where(gy >= 1, 1.0, 0.0).astype(jnp.float32)
        halo_row = jnp.where(lane < 64, plus, minus)

        def column_in(c, per_device, first):
            position = gx * per_device + c - first
            return jnp.where(
                jnp.logical_and(position >= 0, position < n_gx * per_device), 1.0, 0.0
            ).astype(jnp.float32)

        barrier = pltpu.get_barrier_semaphore()
        total = jnp.int32(n_gy - 1)
        for o in range(1, n_gy):
            pl.semaphore_signal(
                barrier, inc=1, device_id=(gx, lax.rem(gy + o, n_gy)), device_id_type=MESH
            )
        for dx, dy in FAR:
            if dx != 0:
                present = there(dx, dy)
                total = total + jnp.where(present, 1, 0)

                @pl.when(present)
                def _():
                    pl.semaphore_signal(
                        barrier, inc=1, device_id=device(dx, dy), device_id_type=MESH
                    )

        for x in range(16):
            v0[0, 8 + x, 0, 8:40, :] = guess[pl.ds(x, 32, stride=16), :]

        def clear(ref, columns, depth, lead=()):
            zero = jnp.zeros((8, 128), jnp.float32)

            def body(c):
                for t in range(2):
                    ref[(*lead, c, t, pl.ds(0, 8), slice(None))] = zero
                    ref[(*lead, c, t, pl.ds(8 + depth, 8), slice(None))] = zero

            loop(0, columns, body, 4)

        for r in range(CYCLES):
            clear(v0, 32, 32, (r,))
        clear(s0, 32, 32)
        clear(s1, 16, 16)
        clear(s2, 8, 8)

        for i, (dx, dy) in enumerate(NEAR):
            @pl.when(jnp.logical_not(there(dx, dy)))
            def _():
                mrx[dx + 1, dy + 1] = jnp.ones((16, 128), jnp.float32)
                for r in range(CYCLES):
                    g2rx[r, dx + 1, dy + 1] = jnp.zeros((4, 8, 128), jnp.float32)
                if dy != 0:
                    for r in range(CYCLES + 1):
                        yrx[r, dx + 1, (dy + 1) // 2] = jnp.zeros((32, 128), jnp.float32)
                else:
                    first = 0 if dx < 0 else 24

                    def body(c):
                        g0[first + c, 0] = jnp.zeros((32, 128), jnp.float32)
                        for r in range(CYCLES):
                            v0[r, first + c, 0, 8:40, :] = jnp.zeros((32, 128), jnp.float32)

                    loop(0, 8, body)
        for dx, dy in FAR:
            @pl.when(jnp.logical_not(there(dx, dy)))
            def _():
                for r in range(CYCLES):
                    g3rx[r, dx + REACH, dy + 1] = jnp.zeros((8, 128), jnp.float32)

        prx[gy] = profile[0]
        mrx[1, 1] = metric[...]
        pl.semaphore_wait(barrier, total)

        def profile_copy(o):
            target = lax.rem(gy + o, n_gy)
            return pltpu.make_async_remote_copy(
                src_ref=profile.at[0], dst_ref=prx.at[gy],
                send_sem=prof_send.at[o], recv_sem=prof_recv.at[o],
                device_id=(gx, target), device_id_type=MESH,
            )

        def profile_arrival(o):
            origin = lax.rem(gy + n_gy - o, n_gy)
            return pltpu.make_async_remote_copy(
                src_ref=profile.at[0], dst_ref=prx.at[origin],
                send_sem=prof_send.at[o], recv_sem=prof_recv.at[o],
                device_id=(gx, origin), device_id_type=MESH,
            )

        for o in range(1, n_gy):
            profile_copy(o).start()

        def near_copy(r, i, arriving, is_g):
            dx, dy = NEAR[i]
            sx, sy = (dx, dy) if arriving else (-dx, -dy)
            slot = i if arriving else len(NEAR) - 1 - i
            if dy == 0:
                here = 8 if dx < 0 else 16
                land = 0 if sx < 0 else 24
                if is_g:
                    src = g0.at[pl.ds(here, 8), 0]
                    dst = g0.at[pl.ds(land, 8), 0]
                else:
                    src = v0.at[r, pl.ds(here, 8), 0, pl.ds(8, 32), :]
                    dst = v0.at[r, pl.ds(land, 8), 0, pl.ds(8, 32), :]
            else:
                src = ytx.at[r]
                dst = yrx.at[r, sx + 1, (sy + 1) // 2]
            return pltpu.make_async_remote_copy(
                src_ref=src, dst_ref=dst,
                send_sem=near_send.at[r, i], recv_sem=near_recv.at[r, slot],
                device_id=device(dx, dy), device_id_type=MESH,
            )

        def block_copy(kind, r, dx, dy, i, count, arriving):
            sx, sy = (dx, dy) if arriving else (-dx, -dy)
            slot = i if arriving else count - 1 - i
            if kind == "m":
                src, dst = metric, mrx.at[sx + 1, sy + 1]
                ss, rs = metric_send.at[i], metric_recv.at[slot]
            elif kind == "g2":
                src, dst = g2tx.at[r], g2rx.at[r, sx + 1, sy + 1]
                ss, rs = g2_send.at[r, i], g2_recv.at[r, slot]
            else:
                src, dst = g3tx.at[r], g3rx.at[r, sx + REACH, sy + 1]
                ss, rs = g3_send.at[r, i], g3_recv.at[r, slot]
            return pltpu.make_async_remote_copy(
                src_ref=src, dst_ref=dst, send_sem=ss, recv_sem=rs,
                device_id=device(dx, dy), device_id_type=MESH,
            )

        def when_there(dx, dy, action):
            @pl.when(there(dx, dy))
            def _():
                action()

        def start_x(r, is_g):
            for i, (dx, dy) in enumerate(NEAR):
                if dy == 0:
                    when_there(dx, dy, lambda: near_copy(r, i, False, is_g).start())

        def start_y(r, load, is_g):
            packed = jnp.zeros((32, 128), jnp.float32)
            for k in range(16):
                turned = pltpu.roll(load(k), (8 * k + 4) % 128, 1)
                packed = jnp.where(lane // 8 == k, turned, packed)
            ytx[r] = packed
            for i, (dx, dy) in enumerate(NEAR):
                if dy != 0:
                    when_there(dx, dy, lambda: near_copy(r, i, False, is_g).start())

        def wait_near(r, is_g):
            for i, (dx, dy) in enumerate(NEAR):
                when_there(dx, dy, lambda: near_copy(r, i, True, is_g).wait_recv())

        def unpack(r, store):
            for dx, first, k0, n in ((-1, 0, 8, 8), (0, 8, 0, 16), (1, 24, 0, 8)):
                both = jnp.where(lane % 8 < 4, yrx[r, dx + 1, 0], yrx[r, dx + 1, 1])
                for j in range(n):
                    shift = (128 - (8 * (k0 + j) + 4)) % 128
                    store(first + j, pltpu.roll(both, shift, 1))

        start_x(0, False)
        for i, (dx, dy) in enumerate(NEAR):
            when_there(
                dx, dy, lambda: block_copy("m", 0, dx, dy, i, len(NEAR), False).start()
            )
        start_y(0, lambda k: v0[0, 8 + k, 0, 8:40, :], False)

        centre0 = coefficients(0)[2]
        for o in range(1, n_gy):
            profile_arrival(o).wait_recv()
        chosen = prx[table[gy]]
        for x in range(16):
            f = source[pl.ds(x, 32, stride=16), :] + chosen[:, x : x + 1] * slope[x : x + 1, :]
            g0[8 + x, 0] = f * (WEIGHT / (metric[x : x + 1, :] * centre0))
        start_x(CYCLES, True)
        start_y(CYCLES, lambda k: g0[8 + k, 0], True)

        for i, (dx, dy) in enumerate(NEAR):
            when_there(
                dx, dy, lambda: block_copy("m", 0, dx, dy, i, len(NEAR), True).wait_recv()
            )
        for c in range(2, 30):
            dx, k = (c - 8) // 16, (c - 8) % 16
            m0[c, 0:1, :] = mrx[dx + 1, 1, k : k + 1, :]
            m0[c, 1:2, :] = jnp.where(
                lane < 64, mrx[dx + 1, 2, k : k + 1, :], mrx[dx + 1, 0, k : k + 1, :]
            )
        for fine, coarse, weights, level, first, span, low, high in (
            (m0, m1, w1, 1, 4, 8, 1, 15),
            (m1, m2, w2, 2, 2, 4, 1, 7),
            (m2, None, w3, 3, 1, 2, 1, 3),
        ):
            centre = coefficients(level)[2]
            for c in range(low, high):
                for t in range(2):
                    row = 0.5 * (
                        fine[2 * c, t : t + 1, :] + fine[2 * c + 1, t : t + 1, :]
                    )
                    if coarse is not None:
                        coarse[c, t : t + 1, :] = row
                    valid = column_in(c, span, first)
                    if t == 1:
                        valid = valid * halo_row
                    weights[c, t : t + 1, :] = valid * (WEIGHT / (row * centre))

        def around(ref, c, depth, grid_level, lead=(), halo=True):
            kx, kz, _ = coefficients(grid_level)

            def at(column, t, shift=0):
                return ref[(*lead, column, t, pl.ds(8 + shift, depth), slice(None))]

            mid, side = at(c, 0), at(c, 1)
            a, b = pltpu.roll(mid, 1, 1), pltpu.roll(side, 1, 1)
            p, q = pltpu.roll(mid, 127, 1), pltpu.roll(side, 127, 1)
            ys = (
                jnp.where(lane == 0, b, a) + jnp.where(lane == 127, q, p),
                jnp.where(lane == 0, a, b) + jnp.where(lane == 127, p, q) if halo else None,
            )
            result = []
            for t in range(2 if halo else 1):
                total = kx * (at(c - 1, t) + at(c + 1, t)) + ys[t]
                total = total + kz * (at(c, t, -1) + at(c, t, 1))
                result.append(((mid, side)[t], total))
            return result

        def weight_of(t, valid, grid_level):
            scale = (WEIGHT / coefficients(grid_level)[2]) * valid
            return scale if t == 0 else scale * halo_row

        def unpack_g(c, value):
            g0[c, 1] = value

        wait_near(CYCLES, True)
        unpack(CYCLES, unpack_g)

        sub = lax.broadcasted_iota(jnp.int32, (8, 128), 0)

        def cycle(r, carry):
            c0, c1, c2, c3 = (coefficients(level)[2] for level in range(4))
            wait_near(r, False)

            def unpack_v(c, value):
                v0[r, c, 1, 8:40, :] = value

            unpack(r, unpack_v)

            def sweep0(c):
                valid = column_in(c, 16, 8)
                for t, (value, nb) in enumerate(around(v0, c, 32, 0, (r,))):
                    s0[c, t, 8:40, :] = 0.2 * value + weight_of(t, valid, 0) * nb + g0[c, t]

            loop(1, 31, sweep0, 2)

            def residual0(c):
                parts = [0.0, 0.0]
                for k in range(2):
                    for t, (value, nb) in enumerate(around(s0, 2 * c + k, 32, 0)):
                        inner = c0 * (1.25 * g0[2 * c + k, t] - value) + nb
                        parts[t] = parts[t] + m0[2 * c + k, t : t + 1, :] * inner
                for t in range(2):
                    r0[c, t] = parts[t]

            loop(1, 15, residual0)

            def restrict0(c):
                for t in range(2):
                    f = r0[c, t, pl.ds(0, 16, stride=2), :] + r0[c, t, pl.ds(1, 16, stride=2), :]
                    g = f * (0.25 * w1[c, t : t + 1, :])
                    g1[c, t] = g
                    s1[c, t, 8:24, :] = g

            loop(1, 15, restrict0, 2)

            def residual1(c):
                parts = [0.0, 0.0]
                for k in range(2):
                    for t, (value, nb) in enumerate(around(s1, 2 * c + k, 16, 1)):
                        inner = (0.25 * c1) * value + nb
                        parts[t] = parts[t] + m1[2 * c + k, t : t + 1, :] * inner
                for t in range(2):
                    r1[c, t] = parts[t]

            loop(1, 7, residual1)

            def restrict1(c):
                for t in range(2):
                    f = r1[c, t, pl.ds(0, 8, stride=2), :] + r1[c, t, pl.ds(1, 8, stride=2), :]
                    s2[c, t, 8:16, :] = f * (0.25 * w2[c, t : t + 1, :])

            for c in range(1, 7):
                restrict1(c)
            for k in range(4):
                own = s2[2 + k, 0, 8:16, :]
                g2tx[r, k] = own
                g2rx[r, 1, 1, k] = own
            for i, (dx, dy) in enumerate(NEAR):
                when_there(
                    dx, dy, lambda: block_copy("g2", r, dx, dy, i, len(NEAR), False).start()
                )
            for c in range(1, 3):
                part = 0.0
                for k in range(2):
                    ((value, nb),) = around(s2, 2 * c + k, 8, 2, halo=False)
                    inner = (0.25 * c2) * value + nb
                    part = part + m2[2 * c + k, 0:1, :] * inner
                r2[c - 1] = part
                f = r2[c - 1, pl.ds(0, 4, stride=2), :] + r2[c - 1, pl.ds(1, 4, stride=2), :]
                g = f * (0.25 * w3[c, 0:1, :])
                g3tx[r, 4 * c - 4 : 4 * c, :] = g
                g3rx[r, REACH, 1, 4 * c - 4 : 4 * c, :] = g
            for i, (dx, dy) in enumerate(FAR):
                when_there(
                    dx, dy, lambda: block_copy("g3", r, dx, dy, i, len(FAR), False).start()
                )
            for i, (dx, dy) in enumerate(FAR):
                when_there(
                    dx, dy, lambda: block_copy("g3", r, dx, dy, i, len(FAR), True).wait_recv()
                )

            kx, kz, _ = coefficients(3)
            width = 2 * REACH + 1
            scale3 = []
            gs = []
            for d in range(width):
                there_x = jnp.logical_and(gx + d - REACH >= 0, gx + d - REACH < n_gx)
                valid = jnp.where(there_x, WEIGHT / c3, 0.0).astype(jnp.float32)
                scale3.append((valid, valid * halo_row))
                gs.append(
                    (g3rx[r, d, 1], jnp.where(lane < 64, g3rx[r, d, 2], g3rx[r, d, 0]))
                )
            zero = jnp.zeros((8, 128), jnp.float32)
            vs = gs
            for sweep in range(SWEEPS):
                new = []
                for d in range(width):
                    mid, side = vs[d]
                    a, b = pltpu.roll(mid, 1, 1), pltpu.roll(side, 1, 1)
                    p, q = pltpu.roll(mid, 127, 1), pltpu.roll(side, 127, 1)
                    ys = (
                        jnp.where(lane == 0, b, a) + jnp.where(lane == 127, q, p),
                        jnp.where(lane == 0, a, b) + jnp.where(lane == 127, p, q),
                    )
                    pair = []
                    for t in range(2):
                        v = vs[d][t]
                        before = vs[d - 1][t] if d > 0 else zero
                        after = vs[d + 1][t] if d + 1 < width else zero
                        xs = pltpu.roll(v + jnp.where(sub >= 4, before, after), 4, 0)
                        zs = jnp.where(sub % 4 != 0, pltpu.roll(v, 1, 0), 0.0)
                        zs = zs + jnp.where(sub % 4 != 3, pltpu.roll(v, 7, 0), 0.0)
                        nb = kx * xs + ys[t] + kz * zs
                        pair.append(0.2 * v + scale3[d][t] * nb + gs[d][t])
                    new.append(tuple(pair))
                vs = new
            for c in range(4):
                d, k = REACH + (c + 1) // 2 - 1, (c + 1) % 2
                for t in range(2):
                    column = vs[d][t][4 * k : 4 * k + 4, :]
                    p3[c, t, pl.ds(0, 4, stride=2), :] = column
                    p3[c, t, pl.ds(1, 4, stride=2), :] = column

            for i, (dx, dy) in enumerate(NEAR):
                when_there(
                    dx, dy, lambda: block_copy("g2", r, dx, dy, i, len(NEAR), True).wait_recv()
                )

            def g2_of(c):
                dx, k = (c - 2) // 4, (c - 2) % 4
                return (
                    g2rx[r, dx + 1, 1, k],
                    jnp.where(lane < 64, g2rx[r, dx + 1, 2, k], g2rx[r, dx + 1, 0, k]),
                )

            for c in range(8):
                g = g2_of(c)
                for t in range(2):
                    s2[c, t, 8:16, :] = g[t] + p3[c // 2, t]
            for c in range(1, 7):
                valid = column_in(c, 4, 2)
                g = g2_of(c)
                for t, (value, nb) in enumerate(around(s2, c, 8, 2)):
                    new = 0.2 * value + weight_of(t, valid, 2) * nb + g[t]
                    p2[c, t, pl.ds(0, 8, stride=2), :] = new
                    p2[c, t, pl.ds(1, 8, stride=2), :] = new

            def correct1(c):
                for k in range(2):
                    for t in range(2):
                        s1[2 * c + k, t, 8:24, :] = g1[2 * c + k, t] + p2[c, t]

            loop(1, 7, correct1, 2)

            def post1(c):
                valid = column_in(c, 8, 4)
                for t, (value, nb) in enumerate(around(s1, c, 16, 1)):
                    new = 0.2 * value + weight_of(t, valid, 1) * nb + g1[c, t]
                    p1[c, t, pl.ds(0, 16, stride=2), :] = new
                    p1[c, t, pl.ds(1, 16, stride=2), :] = new

            loop(3, 13, post1, 2)

            def correct0(c):
                for k in range(2):
                    for t in range(2):
                        old = s0[2 * c + k, t, 8:40, :]
                        s0[2 * c + k, t, 8:40, :] = old + p1[c, t]

            loop(3, 13, correct0)

            def post0(c):
                ((value, nb),) = around(s0, c, 32, 0, halo=False)
                v0[r + 1, c, 0, 8:40, :] = 0.2 * value + (WEIGHT / c0) * nb + g0[c, 0]

            loop(8, 24, post0, 2)

            @pl.when(r + 1 < CYCLES)
            def _():
                start_x(r + 1, False)
                start_y(r + 1, lambda k: v0[r + 1, 8 + k, 0, 8:40, :], False)

            return carry

        lax.fori_loop(0, CYCLES, cycle, 0)

        for x in range(16):
            out[pl.ds(x, 32, stride=16), :] = v0[CYCLES, 8 + x, 0, 8:40, :]

        for o in range(1, n_gy):
            profile_copy(o).wait_send()
        for i, (dx, dy) in enumerate(NEAR):
            def leave():
                block_copy("m", 0, dx, dy, i, len(NEAR), False).wait_send()
                for r in range(CYCLES + 1):
                    near_copy(r, i, False, r == CYCLES).wait_send()
                for r in range(CYCLES):
                    block_copy("g2", r, dx, dy, i, len(NEAR), False).wait_send()

            when_there(dx, dy, leave)
        for i, (dx, dy) in enumerate(FAR):
            def leave():
                for r in range(CYCLES):
                    block_copy("g3", r, dx, dy, i, len(FAR), False).wait_send()

            when_there(dx, dy, leave)

    return kernel


def solution(mesh):
    n_gx, n_gy = mesh.shape["gx"], mesh.shape["gy"]
    f32 = jnp.float32
    near, far = len(NEAR), len(FAR)
    dma = pltpu.SemaphoreType.DMA
    vmem = pl.BlockSpec(memory_space=pltpu.VMEM)
    shapes = [
        (CYCLES + 1, 32, 2, 48, 128),
        (32, 2, 48, 128),
        (32, 2, 32, 128),
        (16, 2, 32, 128),
        (16, 2, 16, 128),
        (8, 2, 24, 128),
        (16, 2, 32, 128),
        (8, 2, 16, 128),
        (2, 8, 128),
        (16, 2, 32, 128),
        (8, 2, 16, 128),
        (4, 2, 8, 128),
        (32, 8, 128),
        (16, 8, 128),
        (8, 8, 128),
        (16, 8, 128),
        (8, 8, 128),
        (4, 8, 128),
        (3, 3, 16, 128),
        (n_gy, 32, 16),
        (CYCLES + 1, 32, 128),
        (CYCLES + 1, 3, 2, 32, 128),
        (CYCLES, 4, 8, 128),
        (CYCLES, 3, 3, 4, 8, 128),
        (CYCLES, 8, 128),
        (CYCLES, 2 * REACH + 1, 3, 8, 128),
    ]
    sems = [
        dma((CYCLES + 1, near)), dma((CYCLES + 1, near)), dma((near,)), dma((near,)),
        dma((CYCLES, near)), dma((CYCLES, near)), dma((CYCLES, far)), dma((CYCLES, far)),
        dma((n_gy,)), dma((n_gy,)),
    ]
    call = pl.pallas_call(
        make_kernel(n_gx, n_gy),
        out_shape=jax.ShapeDtypeStruct((512, 128), f32),
        in_specs=[vmem] * 5 + [pl.BlockSpec(memory_space=pltpu.SMEM)],
        out_specs=vmem,
        scratch_shapes=[pltpu.VMEM(shape, f32) for shape in shapes] + sems,
        compiler_params=pltpu.CompilerParams(
            collective_id=0, has_side_effects=True, vmem_limit_bytes=40 * 1024 * 1024
        ),
    )

    def per_device(source, first_guess, metric, terrain_slope, profile_rows, profile_map):
        result = call(
            source.reshape(512, 128), first_guess.reshape(512, 128),
            metric, terrain_slope, profile_rows, profile_map,
        )
        return result.reshape(source.shape)

    return jax.shard_map(
        per_device,
        mesh=mesh,
        in_specs=(
            P(None, None, "gx", "gy"),
            P(None, None, "gx", "gy"),
            P("gx", "gy"),
            P("gx", "gy"),
            P("gy", None, "gx"),
            P(),
        ),
        out_specs=P(None, None, "gx", "gy"),
        check_vma=False,
    )
```

```python
import jax
import jax.numpy as jnp
from jax import lax
from jax.experimental import pallas as pl
from jax.experimental.pallas import tpu as pltpu
from jax.sharding import PartitionSpec as P

CYCLES = 3
SWEEPS = 5
SIGMA = 0.05
WEIGHT = 0.8
REACH = 3
NEAR = tuple((dx, dy) for dx in (-1, 0, 1) for dy in (-1, 0, 1) if (dx, dy) != (0, 0))
FAR = tuple(
    (dx, dy) for dx in range(-REACH, REACH + 1) for dy in (-1, 0, 1) if (dx, dy) != (0, 0)
)
MESH = pl.DeviceIdType.MESH


def coefficients(grid_level):
    kx = 0.25**grid_level
    kz = 4.0 * kx
    return kx, kz, SIGMA + 2.0 * kx + 2.0 + 2.0 * kz


def loop(low, high, body, step=1):
    count = (high - low) // step

    def several(i, carry):
        for part in range(step):
            body(low + i * step + part)
        return carry

    lax.fori_loop(0, count, several, 0)
    for i in range(low + count * step, high):
        body(i)


def make_kernel(n_gx, n_gy):
    def kernel(
        source, guess, metric, slope, profile, table,
        out,
        v0, s0, f0, g0, s1, g1, s2, r0, r1, r2, p1, p2, p3,
        m0, m1, m2, w1, w2, w3, mtx, mrx, ptx, prx, ytx, yrx, gtx, grx,
        guess_here, source_here,
        near_send, near_recv, metric_send, metric_recv,
        g_send, g_recv, prof_send, prof_recv, local,
    ):
        gx, gy = lax.axis_index("gx"), lax.axis_index("gy")

        def there(dx, dy):
            x, y = gx + dx, gy + dy
            inside = jnp.logical_and(x >= 0, x < n_gx)
            return jnp.logical_and(inside, jnp.logical_and(y >= 0, y < n_gy))

        def device(dx, dy):
            return (gx + dx, gy + dy)

        lane = lax.broadcasted_iota(jnp.int32, (1, 128), 1)
        plus = jnp.where(gy + 1 < n_gy, 1.0, 0.0).astype(jnp.float32)
        minus = jnp.where(gy >= 1, 1.0, 0.0).astype(jnp.float32)
        halo_row = jnp.where(lane < 64, plus, minus)

        def column_in(c, per_device, first):
            position = gx * per_device + c - first
            return jnp.where(
                jnp.logical_and(position >= 0, position < n_gx * per_device), 1.0, 0.0
            ).astype(jnp.float32)

        guess_copy = pltpu.make_async_copy(guess, guess_here, local.at[0])
        source_copy = pltpu.make_async_copy(source, source_here, local.at[1])
        guess_copy.start()
        source_copy.start()

        barrier = pltpu.get_barrier_semaphore()
        total = jnp.int32(n_gy - 1)
        for o in range(1, n_gy):
            pl.semaphore_signal(
                barrier, inc=1, device_id=(gx, lax.rem(gy + o, n_gy)), device_id_type=MESH
            )
        for dx in (-1, 1):
            present = there(dx, 0)
            total = total + jnp.where(present, n_gy, 0)

            @pl.when(present)
            def _():
                for o in range(n_gy):
                    pl.semaphore_signal(
                        barrier, inc=1, device_id=(gx + dx, lax.rem(gy + o, n_gy)),
                        device_id_type=MESH,
                    )
        for dx, dy in FAR:
            if abs(dx) > 1:
                present = there(dx, dy)
                total = total + jnp.where(present, 1, 0)

                @pl.when(present)
                def _():
                    pl.semaphore_signal(
                        barrier, inc=1, device_id=device(dx, dy), device_id_type=MESH
                    )

        def clear(ref, columns, depth, lead=()):
            zero = jnp.zeros((8, 128), jnp.float32)

            def body(c):
                for t in range(2):
                    ref[(*lead, c, t, pl.ds(0, 8), slice(None))] = zero
                    ref[(*lead, c, t, pl.ds(8 + depth, 8), slice(None))] = zero

            loop(0, columns, body, 8)

        for i, (dx, dy) in enumerate(NEAR):
            @pl.when(jnp.logical_not(there(dx, dy)))
            def _():
                mrx[dx + 1, dy + 1] = jnp.ones((32, 128), jnp.float32)
                if dy != 0:
                    for r in range(CYCLES + 1):
                        yrx[r, dx + 1, (dy + 1) // 2] = jnp.zeros((32, 128), jnp.float32)
                else:
                    first = 0 if dx < 0 else 24

                    def body(c):
                        f0[first + c, 0] = jnp.zeros((32, 128), jnp.float32)
                        for r in range(CYCLES):
                            v0[r, first + c, 0, 8:40, :] = jnp.zeros((32, 128), jnp.float32)

                    loop(0, 8, body)
                    prx[dx + 1] = jnp.zeros((n_gy, 32, 16), jnp.float32)
        for dx, dy in FAR:
            @pl.when(jnp.logical_not(there(dx, dy)))
            def _():
                for r in range(CYCLES):
                    grx[r, dx + REACH, dy + 1] = jnp.zeros((40, 128), jnp.float32)

        ptx[...] = profile[0].T
        prx[1, gy] = ptx[...]
        mtx[0:16, :] = metric[...]
        mtx[16:32, :] = slope[...]
        mrx[1, 1] = mtx[...]
        guess_copy.wait()
        for x in range(16):
            v0[0, 8 + x, 0, 8:40, :] = guess_here[pl.ds(x, 32, stride=16), :]
        source_copy.wait()
        for x in range(16):
            f0[8 + x, 0] = source_here[pl.ds(x, 32, stride=16), :]
        pl.semaphore_wait(barrier, total)

        def profile_copy(dx, o, arriving):
            other = lax.rem(gy + (n_gy - o if arriving else o), n_gy)
            sx, sy = (dx, other) if arriving else (-dx, gy)
            return pltpu.make_async_remote_copy(
                src_ref=ptx, dst_ref=prx.at[sx + 1, sy],
                send_sem=prof_send.at[dx + 1, o], recv_sem=prof_recv.at[sx + 1, o],
                device_id=(gx + dx, other), device_id_type=MESH,
            )

        def profile_all(action):
            for dx in (-1, 0, 1):
                @pl.when(there(dx, 0))
                def _():
                    for o in range(1 if dx == 0 else 0, n_gy):
                        action(dx, o)

        def near_copy(r, i, arriving, is_g):
            dx, dy = NEAR[i]
            sx, sy = (dx, dy) if arriving else (-dx, -dy)
            slot = i if arriving else len(NEAR) - 1 - i
            if dy == 0:
                here = 8 if dx < 0 else 16
                land = 0 if sx < 0 else 24
                if is_g:
                    src = f0.at[pl.ds(here, 8), 0]
                    dst = f0.at[pl.ds(land, 8), 0]
                else:
                    src = v0.at[r, pl.ds(here, 8), 0, pl.ds(8, 32), :]
                    dst = v0.at[r, pl.ds(land, 8), 0, pl.ds(8, 32), :]
            else:
                src = ytx.at[r]
                dst = yrx.at[r, sx + 1, (sy + 1) // 2]
            return pltpu.make_async_remote_copy(
                src_ref=src, dst_ref=dst,
                send_sem=near_send.at[r, i], recv_sem=near_recv.at[r, slot],
                device_id=device(dx, dy), device_id_type=MESH,
            )

        def block_copy(kind, r, dx, dy, i, count, arriving):
            sx, sy = (dx, dy) if arriving else (-dx, -dy)
            slot = i if arriving else count - 1 - i
            if kind == "m":
                src, dst = mtx, mrx.at[sx + 1, sy + 1]
                ss, rs = metric_send.at[i], metric_recv.at[slot]
            else:
                rows = pl.ds(0, 40) if abs(dx) < 2 else pl.ds(32, 8)
                src, dst = gtx.at[r, rows], grx.at[r, sx + REACH, sy + 1, rows]
                ss, rs = g_send.at[r, i], g_recv.at[r, slot]
            return pltpu.make_async_remote_copy(
                src_ref=src, dst_ref=dst, send_sem=ss, recv_sem=rs,
                device_id=device(dx, dy), device_id_type=MESH,
            )

        def when_there(dx, dy, action):
            @pl.when(there(dx, dy))
            def _():
                action()

        def start_x(r, is_g, sides=(-1, 1)):
            for i, (dx, dy) in enumerate(NEAR):
                if dy == 0 and dx in sides:
                    when_there(dx, dy, lambda: near_copy(r, i, False, is_g).start())

        def start_y(r, load, is_g):
            packed = jnp.zeros((32, 128), jnp.float32)
            for k in range(16):
                turned = pltpu.roll(load(k), (8 * k + 4) % 128, 1)
                packed = jnp.where(lane // 8 == k, turned, packed)
            ytx[r] = packed
            for i, (dx, dy) in enumerate(NEAR):
                if dy != 0:
                    when_there(dx, dy, lambda: near_copy(r, i, False, is_g).start())

        def wait_near(r, is_g, direct=None):
            for i, (dx, dy) in enumerate(NEAR):
                if direct is not None and direct != (dx == 0):
                    continue
                when_there(dx, dy, lambda: near_copy(r, i, True, is_g).wait_recv())

        def unpack(r, store, parts=(-1, 0, 1)):
            for dx, first, k0, n in ((-1, 0, 8, 8), (0, 8, 0, 16), (1, 24, 0, 8)):
                if dx not in parts:
                    continue
                both = jnp.where(lane % 8 < 4, yrx[r, dx + 1, 0], yrx[r, dx + 1, 1])
                for j in range(n):
                    shift = (128 - (8 * (k0 + j) + 4)) % 128
                    store(first + j, pltpu.roll(both, shift, 1))

        start_x(0, False)
        start_x(CYCLES, True)
        profile_all(lambda dx, o: profile_copy(dx, o, False).start())
        for i, (dx, dy) in enumerate(NEAR):
            when_there(
                dx, dy, lambda: block_copy("m", 0, dx, dy, i, len(NEAR), False).start()
            )
        start_y(0, lambda k: v0[0, 8 + k, 0, 8:40, :], False)
        start_y(CYCLES, lambda k: f0[8 + k, 0], True)

        for r in range(CYCLES):
            clear(v0, 32, 32, (r,))
        clear(s0, 32, 32)
        clear(s1, 16, 16)
        clear(s2, 8, 8)

        for i, (dx, dy) in enumerate(NEAR):
            when_there(
                dx, dy, lambda: block_copy("m", 0, dx, dy, i, len(NEAR), True).wait_recv()
            )
        for c in range(32):
            dx, k = (c - 8) // 16, (c - 8) % 16
            m0[c, 0:1, :] = mrx[dx + 1, 1, k : k + 1, :]
            m0[c, 1:2, :] = jnp.where(
                lane < 64, mrx[dx + 1, 2, k : k + 1, :], mrx[dx + 1, 0, k : k + 1, :]
            )
        for fine, coarse, weights, level, first, span, low, high in (
            (m0, m1, w1, 1, 4, 8, 1, 15),
            (m1, m2, w2, 2, 2, 4, 1, 7),
            (m2, None, w3, 3, 1, 2, 1, 3),
        ):
            centre = coefficients(level)[2]
            for c in range(low, high):
                for t in range(2):
                    row = 0.5 * (
                        fine[2 * c, t : t + 1, :] + fine[2 * c + 1, t : t + 1, :]
                    )
                    if coarse is not None:
                        coarse[c, t : t + 1, :] = row
                    valid = column_in(c, span, first)
                    if t == 1:
                        valid = valid * halo_row
                    weights[c, t : t + 1, :] = valid * (WEIGHT / (row * centre))

        def around(ref, c, depth, grid_level, lead=(), halo=True):
            kx, kz, _ = coefficients(grid_level)

            def at(column, t, shift=0):
                return ref[(*lead, column, t, pl.ds(8 + shift, depth), slice(None))]

            mid, side = at(c, 0), at(c, 1)
            a, b = pltpu.roll(mid, 1, 1), pltpu.roll(side, 1, 1)
            p, q = pltpu.roll(mid, 127, 1), pltpu.roll(side, 127, 1)
            ys = (
                jnp.where(lane == 0, b, a) + jnp.where(lane == 127, q, p),
                jnp.where(lane == 0, a, b) + jnp.where(lane == 127, p, q) if halo else None,
            )
            result = []
            for t in range(2 if halo else 1):
                total = kx * (at(c - 1, t) + at(c + 1, t)) + ys[t]
                total = total + kz * (at(c, t, -1) + at(c, t, 1))
                result.append(((mid, side)[t], total))
            return result

        def weight_of(t, valid, grid_level):
            scale = (WEIGHT / coefficients(grid_level)[2]) * valid
            return scale if t == 0 else scale * halo_row

        def unpack_g(c, value):
            f0[c, 1] = value

        profile_all(lambda dx, o: profile_copy(dx, o, True).wait_recv())
        wait_near(CYCLES, True)
        unpack(CYCLES, unpack_g)
        centre0 = coefficients(0)[2]
        strips = (
            table[gy], table[jnp.minimum(gy + 1, n_gy - 1)], table[jnp.maximum(gy - 1, 0)]
        )
        for dx, first, k0, n in ((-1, 0, 8, 8), (0, 8, 0, 16), (1, 24, 0, 8)):
            own, above, below = (prx[dx + 1, strip] for strip in strips)
            for j in range(n):
                c, k = first + j, k0 + j
                column = slice(k, k + 1)
                row = 16 + k
                valid = column_in(c, 16, 8) * (WEIGHT / centre0)
                g0[c, 0] = (f0[c, 0] + own[:, column] * mrx[dx + 1, 1, row : row + 1, :]) * (
                    valid / m0[c, 0:1, :]
                )
                side = jnp.where(lane < 64, above[:, column], below[:, column])
                steep = jnp.where(
                    lane < 64, mrx[dx + 1, 2, row : row + 1, :], mrx[dx + 1, 0, row : row + 1, :]
                )
                g0[c, 1] = (f0[c, 1] + side * steep) * (valid * halo_row / m0[c, 1:2, :])

        def g_copy(r, dx, dy, i, arriving):
            return block_copy("g", r, dx, dy, i, len(FAR), arriving)

        def far_all(action):
            for i, (dx, dy) in enumerate(FAR):
                when_there(dx, dy, lambda: action(dx, dy, i))

        sub = lax.broadcasted_iota(jnp.int32, (8, 128), 0)

        def cycle(r, carry):
            c0, c1, c2, c3 = (coefficients(level)[2] for level in range(4))
            def unpack_v(c, value):
                v0[r, c, 1, 8:40, :] = value

            def sweep0(c):
                valid = column_in(c, 16, 8)
                for t, (value, nb) in enumerate(around(v0, c, 32, 0, (r,))):
                    s0[c, t, 8:40, :] = 0.2 * value + weight_of(t, valid, 0) * nb + g0[c, t]

            def residual0(c):
                parts = [0.0, 0.0]
                for k in range(2):
                    for t, (value, nb) in enumerate(around(s0, 2 * c + k, 32, 0)):
                        inner = c0 * (1.25 * g0[2 * c + k, t] - value) + nb
                        parts[t] = parts[t] + m0[2 * c + k, t : t + 1, :] * inner
                for t in range(2):
                    r0[c, t] = parts[t]

            wait_near(r, False, True)
            unpack(r, unpack_v, (0,))
            loop(9, 23, sweep0, 7)
            loop(5, 11, residual0, 3)

            @pl.when(r > 0)
            def _():
                far_all(lambda dx, dy, i: g_copy(r - 1, dx, dy, i, False).wait_send())

            wait_near(r, False, False)
            unpack(r, unpack_v, (-1, 1))
            for low in (1, 23):
                loop(low, low + 8, sweep0, 8)
            for low in (1, 11):
                loop(low, low + 4, residual0, 4)

            def restrict0(c):
                for t in range(2):
                    f = r0[c, t, pl.ds(0, 16, stride=2), :] + r0[c, t, pl.ds(1, 16, stride=2), :]
                    g = f * (0.25 * w1[c, t : t + 1, :])
                    g1[c, t] = g
                    s1[c, t, 8:24, :] = g

            loop(1, 15, restrict0, 7)

            def residual1(c):
                parts = [0.0, 0.0]
                for k in range(2):
                    for t, (value, nb) in enumerate(around(s1, 2 * c + k, 16, 1)):
                        inner = (0.25 * c1) * value + nb
                        parts[t] = parts[t] + m1[2 * c + k, t : t + 1, :] * inner
                for t in range(2):
                    r1[c, t] = parts[t]

            loop(1, 7, residual1, 3)

            def restrict1(c):
                for t in range(2):
                    f = r1[c, t, pl.ds(0, 8, stride=2), :] + r1[c, t, pl.ds(1, 8, stride=2), :]
                    s2[c, t, 8:16, :] = f * (0.25 * w2[c, t : t + 1, :])

            for c in range(1, 7):
                restrict1(c)
            for k in range(4):
                own = s2[2 + k, 0, 8:16, :]
                gtx[r, 8 * k : 8 * k + 8, :] = own
                grx[r, REACH, 1, 8 * k : 8 * k + 8, :] = own
            for c in range(1, 3):
                part = 0.0
                for k in range(2):
                    ((value, nb),) = around(s2, 2 * c + k, 8, 2, halo=False)
                    inner = (0.25 * c2) * value + nb
                    part = part + m2[2 * c + k, 0:1, :] * inner
                r2[c - 1] = part
                f = r2[c - 1, pl.ds(0, 4, stride=2), :] + r2[c - 1, pl.ds(1, 4, stride=2), :]
                g = f * (0.25 * w3[c, 0:1, :])
                gtx[r, 28 + 4 * c : 32 + 4 * c, :] = g
                grx[r, REACH, 1, 28 + 4 * c : 32 + 4 * c, :] = g
            far_all(lambda dx, dy, i: g_copy(r, dx, dy, i, False).start())

            for i, (dx, dy) in enumerate(NEAR):
                when_there(dx, dy, lambda: near_copy(r, i, False, False).wait_send())

            @pl.when(r == 0)
            def _():
                profile_all(lambda dx, o: profile_copy(dx, o, False).wait_send())
                for i, (dx, dy) in enumerate(NEAR):
                    def leave():
                        block_copy("m", 0, dx, dy, i, len(NEAR), False).wait_send()
                        near_copy(CYCLES, i, False, True).wait_send()

                    when_there(dx, dy, leave)

            far_all(lambda dx, dy, i: g_copy(r, dx, dy, i, True).wait_recv())

            kx, kz, _ = coefficients(3)
            width = 2 * REACH + 1
            scale3 = []
            gs = []
            for d in range(width):
                there_x = jnp.logical_and(gx + d - REACH >= 0, gx + d - REACH < n_gx)
                valid = jnp.where(there_x, WEIGHT / c3, 0.0).astype(jnp.float32)
                scale3.append((valid, valid * halo_row))
                gs.append(
                    (
                        grx[r, d, 1, 32:40, :],
                        jnp.where(lane < 64, grx[r, d, 2, 32:40, :], grx[r, d, 0, 32:40, :]),
                    )
                )
            zero = jnp.zeros((8, 128), jnp.float32)
            vs = gs
            for sweep in range(SWEEPS):
                new = []
                for d in range(width):
                    mid, side = vs[d]
                    a, b = pltpu.roll(mid, 1, 1), pltpu.roll(side, 1, 1)
                    p, q = pltpu.roll(mid, 127, 1), pltpu.roll(side, 127, 1)
                    ys = (
                        jnp.where(lane == 0, b, a) + jnp.where(lane == 127, q, p),
                        jnp.where(lane == 0, a, b) + jnp.where(lane == 127, p, q),
                    )
                    pair = []
                    for t in range(2):
                        v = vs[d][t]
                        before = vs[d - 1][t] if d > 0 else zero
                        after = vs[d + 1][t] if d + 1 < width else zero
                        xs = pltpu.roll(v + jnp.where(sub >= 4, before, after), 4, 0)
                        zs = jnp.where(sub % 4 != 0, pltpu.roll(v, 1, 0), 0.0)
                        zs = zs + jnp.where(sub % 4 != 3, pltpu.roll(v, 7, 0), 0.0)
                        nb = kx * xs + ys[t] + kz * zs
                        pair.append(0.2 * v + scale3[d][t] * nb + gs[d][t])
                    new.append(tuple(pair))
                vs = new
            for c in range(4):
                d, k = REACH + (c + 1) // 2 - 1, (c + 1) % 2
                for t in range(2):
                    column = vs[d][t][4 * k : 4 * k + 4, :]
                    p3[c, t, pl.ds(0, 4, stride=2), :] = column
                    p3[c, t, pl.ds(1, 4, stride=2), :] = column

            def g2_of(c):
                d, k = (c - 2) // 4 + REACH, (c - 2) % 4
                rows = slice(8 * k, 8 * k + 8)
                return (
                    grx[r, d, 1, rows, :],
                    jnp.where(lane < 64, grx[r, d, 2, rows, :], grx[r, d, 0, rows, :]),
                )

            for c in range(8):
                g = g2_of(c)
                for t in range(2):
                    s2[c, t, 8:16, :] = g[t] + p3[c // 2, t]
            for c in range(1, 7):
                valid = column_in(c, 4, 2)
                g = g2_of(c)
                for t, (value, nb) in enumerate(around(s2, c, 8, 2)):
                    new = 0.2 * value + weight_of(t, valid, 2) * nb + g[t]
                    p2[c, t, pl.ds(0, 8, stride=2), :] = new
                    p2[c, t, pl.ds(1, 8, stride=2), :] = new

            def correct1(c):
                for k in range(2):
                    for t in range(2):
                        s1[2 * c + k, t, 8:24, :] = g1[2 * c + k, t] + p2[c, t]

            loop(1, 7, correct1, 6)

            def post1(c):
                valid = column_in(c, 8, 4)
                for t, (value, nb) in enumerate(around(s1, c, 16, 1)):
                    new = 0.2 * value + weight_of(t, valid, 1) * nb + g1[c, t]
                    p1[c, t, pl.ds(0, 16, stride=2), :] = new
                    p1[c, t, pl.ds(1, 16, stride=2), :] = new

            loop(3, 13, post1, 5)

            def correct0(c):
                for k in range(2):
                    for t in range(2):
                        old = s0[2 * c + k, t, 8:40, :]
                        s0[2 * c + k, t, 8:40, :] = old + p1[c, t]

            loop(3, 13, correct0, 2)

            def post0(c):
                ((value, nb),) = around(s0, c, 32, 0, halo=False)
                v0[r + 1, c, 0, 8:40, :] = 0.2 * value + (WEIGHT / c0) * nb + g0[c, 0]

            loop(8, 16, post0, 8)

            @pl.when(r + 1 < CYCLES)
            def _():
                start_x(r + 1, False, (-1,))

            loop(16, 24, post0, 8)

            @pl.when(r + 1 < CYCLES)
            def _():
                start_x(r + 1, False, (1,))
                start_y(r + 1, lambda k: v0[r + 1, 8 + k, 0, 8:40, :], False)

            return carry

        lax.fori_loop(0, CYCLES, cycle, 0)

        for x in range(16):
            out[pl.ds(x, 32, stride=16), :] = v0[CYCLES, 8 + x, 0, 8:40, :]

        far_all(lambda dx, dy, i: g_copy(CYCLES - 1, dx, dy, i, False).wait_send())

    return kernel


def solution(mesh):
    n_gx, n_gy = mesh.shape["gx"], mesh.shape["gy"]
    f32 = jnp.float32
    near, far = len(NEAR), len(FAR)
    dma = pltpu.SemaphoreType.DMA
    vmem = pl.BlockSpec(memory_space=pltpu.VMEM)
    shapes = [
        (CYCLES + 1, 32, 2, 48, 128),
        (32, 2, 48, 128),
        (32, 2, 32, 128),
        (32, 2, 32, 128),
        (16, 2, 32, 128),
        (16, 2, 16, 128),
        (8, 2, 24, 128),
        (16, 2, 32, 128),
        (8, 2, 16, 128),
        (2, 8, 128),
        (16, 2, 32, 128),
        (8, 2, 16, 128),
        (4, 2, 8, 128),
        (32, 8, 128),
        (16, 8, 128),
        (8, 8, 128),
        (16, 8, 128),
        (8, 8, 128),
        (4, 8, 128),
        (32, 128),
        (3, 3, 32, 128),
        (32, 16),
        (3, n_gy, 32, 16),
        (CYCLES + 1, 32, 128),
        (CYCLES + 1, 3, 2, 32, 128),
        (CYCLES, 40, 128),
        (CYCLES, 2 * REACH + 1, 3, 40, 128),
        (512, 128),
        (512, 128),
    ]
    sems = [
        dma((CYCLES + 1, near)), dma((CYCLES + 1, near)), dma((near,)), dma((near,)),
        dma((CYCLES, far)), dma((CYCLES, far)), dma((3, n_gy)), dma((3, n_gy)), dma((2,)),
    ]
    call = pl.pallas_call(
        make_kernel(n_gx, n_gy),
        out_shape=jax.ShapeDtypeStruct((512, 128), f32),
        in_specs=[pl.BlockSpec(memory_space=pltpu.HBM)] * 2 + [vmem] * 3 + [pl.BlockSpec(memory_space=pltpu.SMEM)],
        out_specs=vmem,
        scratch_shapes=[pltpu.VMEM(shape, f32) for shape in shapes] + sems,
        compiler_params=pltpu.CompilerParams(
            collective_id=0, has_side_effects=True, vmem_limit_bytes=62 * 1024 * 1024
        ),
    )

    def per_device(source, first_guess, metric, terrain_slope, profile_rows, profile_map):
        result = call(
            source.reshape(512, 128), first_guess.reshape(512, 128),
            metric, terrain_slope, jnp.swapaxes(profile_rows, 1, 2), profile_map,
        )
        return result.reshape(source.shape)

    return jax.shard_map(
        per_device,
        mesh=mesh,
        in_specs=(
            P(None, None, "gx", "gy"),
            P(None, None, "gx", "gy"),
            P("gx", "gy"),
            P("gx", "gy"),
            P("gy", None, "gx"),
            P(),
        ),
        out_specs=P(None, None, "gx", "gy"),
        check_vma=False,
    )
```

```python
import jax
import jax.numpy as jnp
from jax import lax
from jax.experimental import pallas as pl
from jax.experimental.pallas import tpu as pltpu
from jax.sharding import PartitionSpec as P

CYCLES = 3
SWEEPS = 5
SIGMA = 0.05
WEIGHT = 0.8
REACH = 3
NEAR = tuple((dx, dy) for dx in (-1, 0, 1) for dy in (-1, 0, 1) if (dx, dy) != (0, 0))
FAR = tuple(
    (dx, dy) for dx in range(-REACH, REACH + 1) for dy in (-1, 0, 1) if (dx, dy) != (0, 0)
)
MESH = pl.DeviceIdType.MESH


def coefficients(grid_level):
    kx = 0.25**grid_level
    kz = 4.0 * kx
    return kx, kz, SIGMA + 2.0 * kx + 2.0 + 2.0 * kz


def loop(low, high, body, step=1):
    count = (high - low) // step

    def several(i, carry):
        for part in range(step):
            body(low + i * step + part)
        return carry

    lax.fori_loop(0, count, several, 0)
    for i in range(low + count * step, high):
        body(i)


def make_kernel(n_gx, n_gy):
    def kernel(
        source, guess, metric, slope, profile, table,
        out,
        v0, s0, f0, g0, s1, g1, s2, r0, r1, r2, p1, p2, p3,
        m0, m1, m2, w1, w2, w3, mtx, mrx, ptx, prx, ytx, yrx, gtx, grx,
        guess_here, source_here,
        near_send, near_recv, metric_send, metric_recv,
        g_send, g_recv, prof_send, prof_recv, local,
    ):
        gx, gy = lax.axis_index("gx"), lax.axis_index("gy")

        def there(dx, dy):
            x, y = gx + dx, gy + dy
            inside = jnp.logical_and(x >= 0, x < n_gx)
            return jnp.logical_and(inside, jnp.logical_and(y >= 0, y < n_gy))

        def device(dx, dy):
            return (gx + dx, gy + dy)

        lane = lax.broadcasted_iota(jnp.int32, (1, 128), 1)
        plus = jnp.where(gy + 1 < n_gy, 1.0, 0.0).astype(jnp.float32)
        minus = jnp.where(gy >= 1, 1.0, 0.0).astype(jnp.float32)
        halo_row = jnp.where(lane < 64, plus, minus)

        def column_in(c, per_device, first):
            position = gx * per_device + c - first
            return jnp.where(
                jnp.logical_and(position >= 0, position < n_gx * per_device), 1.0, 0.0
            ).astype(jnp.float32)

        guess_copy = pltpu.make_async_copy(guess, guess_here, local.at[0])
        source_copy = pltpu.make_async_copy(source, source_here, local.at[1])
        guess_copy.start()
        source_copy.start()

        barrier = pltpu.get_barrier_semaphore()
        total = jnp.int32(n_gy - 1)
        for o in range(1, n_gy):
            pl.semaphore_signal(
                barrier, inc=1, device_id=(gx, lax.rem(gy + o, n_gy)), device_id_type=MESH
            )
        for dx in (-1, 1):
            present = there(dx, 0)
            total = total + jnp.where(present, n_gy, 0)

            @pl.when(present)
            def _():
                for o in range(n_gy):
                    pl.semaphore_signal(
                        barrier, inc=1, device_id=(gx + dx, lax.rem(gy + o, n_gy)),
                        device_id_type=MESH,
                    )
        for dx, dy in FAR:
            if abs(dx) > 1:
                present = there(dx, dy)
                total = total + jnp.where(present, 1, 0)

                @pl.when(present)
                def _():
                    pl.semaphore_signal(
                        barrier, inc=1, device_id=device(dx, dy), device_id_type=MESH
                    )

        def clear(ref, columns, depth, lead=()):
            zero = jnp.zeros((8, 128), jnp.float32)

            def body(c):
                for t in range(2):
                    ref[(*lead, c, t, pl.ds(0, 8), slice(None))] = zero
                    ref[(*lead, c, t, pl.ds(8 + depth, 8), slice(None))] = zero

            loop(0, columns, body, 8)

        for i, (dx, dy) in enumerate(NEAR):
            @pl.when(jnp.logical_not(there(dx, dy)))
            def _():
                mrx[dx + 1, dy + 1] = jnp.ones((32, 128), jnp.float32)
                if dy != 0:
                    for r in range(CYCLES + 1):
                        yrx[r, dx + 1, (dy + 1) // 2] = jnp.zeros((32, 128), jnp.float32)
                else:
                    first = 0 if dx < 0 else 24

                    def body(c):
                        f0[first + c, 0] = jnp.zeros((32, 128), jnp.float32)
                        for r in range(CYCLES):
                            v0[r, first + c, 0, 8:40, :] = jnp.zeros((32, 128), jnp.float32)

                    loop(0, 8, body)
                    prx[dx + 1] = jnp.zeros((n_gy, 32, 16), jnp.float32)
        for dx, dy in FAR:
            @pl.when(jnp.logical_not(there(dx, dy)))
            def _():
                for r in range(CYCLES):
                    grx[r, dx + REACH, dy + 1] = jnp.zeros((48, 128), jnp.float32)

        ptx[...] = profile[0].T
        prx[1, gy] = ptx[...]
        mtx[0:16, :] = metric[...]
        mtx[16:32, :] = slope[...]
        mrx[1, 1] = mtx[...]
        guess_copy.wait()
        for x in range(16):
            v0[0, 8 + x, 0, 8:40, :] = guess_here[pl.ds(x, 32, stride=16), :]
        source_copy.wait()
        for x in range(16):
            f0[8 + x, 0] = source_here[pl.ds(x, 32, stride=16), :]
        pl.semaphore_wait(barrier, total)

        def profile_copy(dx, o, arriving):
            other = lax.rem(gy + (n_gy - o if arriving else o), n_gy)
            sx, sy = (dx, other) if arriving else (-dx, gy)
            return pltpu.make_async_remote_copy(
                src_ref=ptx, dst_ref=prx.at[sx + 1, sy],
                send_sem=prof_send.at[dx + 1, o], recv_sem=prof_recv.at[sx + 1, o],
                device_id=(gx + dx, other), device_id_type=MESH,
            )

        def profile_all(action):
            for dx in (-1, 0, 1):
                @pl.when(there(dx, 0))
                def _():
                    for o in range(1 if dx == 0 else 0, n_gy):
                        action(dx, o)

        def near_copy(r, i, arriving, is_g):
            dx, dy = NEAR[i]
            sx, sy = (dx, dy) if arriving else (-dx, -dy)
            slot = i if arriving else len(NEAR) - 1 - i
            if dy == 0:
                here = 8 if dx < 0 else 16
                land = 0 if sx < 0 else 24
                if is_g:
                    src = f0.at[pl.ds(here, 8), 0]
                    dst = f0.at[pl.ds(land, 8), 0]
                else:
                    src = v0.at[r, pl.ds(here, 8), 0, pl.ds(8, 32), :]
                    dst = v0.at[r, pl.ds(land, 8), 0, pl.ds(8, 32), :]
            else:
                src = ytx.at[r]
                dst = yrx.at[r, sx + 1, (sy + 1) // 2]
            return pltpu.make_async_remote_copy(
                src_ref=src, dst_ref=dst,
                send_sem=near_send.at[r, i], recv_sem=near_recv.at[r, slot],
                device_id=device(dx, dy), device_id_type=MESH,
            )

        def block_copy(kind, r, dx, dy, i, count, arriving):
            sx, sy = (dx, dy) if arriving else (-dx, -dy)
            slot = i if arriving else count - 1 - i
            if kind == "m":
                src, dst = mtx, mrx.at[sx + 1, sy + 1]
                ss, rs = metric_send.at[i], metric_recv.at[slot]
            else:
                step = -dx if arriving else dx
                rows = {-1: pl.ds(0, 24), 0: pl.ds(0, 40), 1: pl.ds(24, 24)}.get(
                    step, pl.ds(0, 8)
                )
                src, dst = gtx.at[r, rows], grx.at[r, sx + REACH, sy + 1, rows]
                ss, rs = g_send.at[r, i], g_recv.at[r, slot]
            return pltpu.make_async_remote_copy(
                src_ref=src, dst_ref=dst, send_sem=ss, recv_sem=rs,
                device_id=device(dx, dy), device_id_type=MESH,
            )

        def when_there(dx, dy, action):
            @pl.when(there(dx, dy))
            def _():
                action()

        def start_x(r, is_g, sides=(-1, 1)):
            for i, (dx, dy) in enumerate(NEAR):
                if dy == 0 and dx in sides:
                    when_there(dx, dy, lambda: near_copy(r, i, False, is_g).start())

        def start_y(r, load, is_g):
            packed = jnp.zeros((32, 128), jnp.float32)
            for k in range(16):
                turned = pltpu.roll(load(k), (8 * k + 4) % 128, 1)
                packed = jnp.where(lane // 8 == k, turned, packed)
            ytx[r] = packed
            for i, (dx, dy) in enumerate(NEAR):
                if dy != 0:
                    when_there(dx, dy, lambda: near_copy(r, i, False, is_g).start())

        def wait_near(r, is_g, direct=None):
            for i, (dx, dy) in enumerate(NEAR):
                if direct is not None and direct != (dx == 0):
                    continue
                when_there(dx, dy, lambda: near_copy(r, i, True, is_g).wait_recv())

        def unpack(r, store, parts=(-1, 0, 1)):
            for dx, first, k0, n in ((-1, 0, 8, 8), (0, 8, 0, 16), (1, 24, 0, 8)):
                if dx not in parts:
                    continue
                both = jnp.where(lane % 8 < 4, yrx[r, dx + 1, 0], yrx[r, dx + 1, 1])
                for j in range(n):
                    shift = (128 - (8 * (k0 + j) + 4)) % 128
                    store(first + j, pltpu.roll(both, shift, 1))

        profile_all(lambda dx, o: profile_copy(dx, o, False).start())
        for i, (dx, dy) in enumerate(NEAR):
            when_there(
                dx, dy, lambda: block_copy("m", 0, dx, dy, i, len(NEAR), False).start()
            )
        start_x(0, False)
        start_x(CYCLES, True)
        start_y(CYCLES, lambda k: f0[8 + k, 0], True)
        start_y(0, lambda k: v0[0, 8 + k, 0, 8:40, :], False)

        for r in range(CYCLES):
            clear(v0, 32, 32, (r,))
        clear(s0, 32, 32)
        clear(s1, 16, 16)
        clear(s2, 8, 8)

        for i, (dx, dy) in enumerate(NEAR):
            when_there(
                dx, dy, lambda: block_copy("m", 0, dx, dy, i, len(NEAR), True).wait_recv()
            )
        for c in range(32):
            dx, k = (c - 8) // 16, (c - 8) % 16
            m0[c, 0:1, :] = mrx[dx + 1, 1, k : k + 1, :]
            m0[c, 1:2, :] = jnp.where(
                lane < 64, mrx[dx + 1, 2, k : k + 1, :], mrx[dx + 1, 0, k : k + 1, :]
            )
        for fine, coarse, weights, level, first, span, low, high in (
            (m0, m1, w1, 1, 4, 8, 1, 15),
            (m1, m2, w2, 2, 2, 4, 1, 7),
            (m2, None, w3, 3, 1, 2, 1, 3),
        ):
            centre = coefficients(level)[2]
            for c in range(low, high):
                for t in range(2):
                    row = 0.5 * (
                        fine[2 * c, t : t + 1, :] + fine[2 * c + 1, t : t + 1, :]
                    )
                    if coarse is not None:
                        coarse[c, t : t + 1, :] = row
                    valid = column_in(c, span, first)
                    if t == 1:
                        valid = valid * halo_row
                    weights[c, t : t + 1, :] = valid * (WEIGHT / (row * centre))

        def around(ref, c, depth, grid_level, lead=(), halo=True):
            kx, kz, _ = coefficients(grid_level)

            def at(column, t, shift=0):
                return ref[(*lead, column, t, pl.ds(8 + shift, depth), slice(None))]

            mid, side = at(c, 0), at(c, 1)
            a, b = pltpu.roll(mid, 1, 1), pltpu.roll(side, 1, 1)
            p, q = pltpu.roll(mid, 127, 1), pltpu.roll(side, 127, 1)
            ys = (
                jnp.where(lane == 0, b, a) + jnp.where(lane == 127, q, p),
                jnp.where(lane == 0, a, b) + jnp.where(lane == 127, p, q) if halo else None,
            )
            result = []
            for t in range(2 if halo else 1):
                total = kx * (at(c - 1, t) + at(c + 1, t)) + ys[t]
                total = total + kz * (at(c, t, -1) + at(c, t, 1))
                result.append(((mid, side)[t], total))
            return result

        def weight_of(t, valid, grid_level):
            scale = (WEIGHT / coefficients(grid_level)[2]) * valid
            return scale if t == 0 else scale * halo_row

        def unpack_g(c, value):
            f0[c, 1] = value

        centre0 = coefficients(0)[2]

        def right_side(parts):
            for dx, first, k0, n in ((-1, 0, 8, 8), (0, 8, 0, 16), (1, 24, 0, 8)):
                if dx not in parts:
                    continue
                own, above, below = (
                    prx[dx + 1, strip]
                    for strip in (
                        table[gy],
                        table[jnp.minimum(gy + 1, n_gy - 1)],
                        table[jnp.maximum(gy - 1, 0)],
                    )
                )
                for j in range(n):
                    c, k = first + j, k0 + j
                    column = slice(k, k + 1)
                    row = 16 + k
                    valid = column_in(c, 16, 8) * (WEIGHT / centre0)
                    g0[c, 0] = (f0[c, 0] + own[:, column] * mrx[dx + 1, 1, row : row + 1, :]) * (
                        valid / m0[c, 0:1, :]
                    )
                    side = jnp.where(lane < 64, above[:, column], below[:, column])
                    steep = jnp.where(
                        lane < 64, mrx[dx + 1, 2, row : row + 1, :], mrx[dx + 1, 0, row : row + 1, :]
                    )
                    g0[c, 1] = (f0[c, 1] + side * steep) * (valid * halo_row / m0[c, 1:2, :])

        profile_all(lambda dx, o: profile_copy(dx, o, True).wait_recv())
        wait_near(CYCLES, True, True)
        unpack(CYCLES, unpack_g, (0,))
        right_side((0,))

        def g_copy(r, dx, dy, i, arriving):
            return block_copy("g", r, dx, dy, i, len(FAR), arriving)

        def far_all(action):
            for i, (dx, dy) in enumerate(FAR):
                when_there(dx, dy, lambda: action(dx, dy, i))

        sub = lax.broadcasted_iota(jnp.int32, (8, 128), 0)

        def cycle(r, carry):
            c0, c1, c2, c3 = (coefficients(level)[2] for level in range(4))
            def unpack_v(c, value):
                v0[r, c, 1, 8:40, :] = value

            def sweep0(c):
                valid = column_in(c, 16, 8)
                for t, (value, nb) in enumerate(around(v0, c, 32, 0, (r,))):
                    s0[c, t, 8:40, :] = 0.2 * value + weight_of(t, valid, 0) * nb + g0[c, t]

            def residual0(c):
                parts = [0.0, 0.0]
                for k in range(2):
                    for t, (value, nb) in enumerate(around(s0, 2 * c + k, 32, 0)):
                        inner = c0 * (1.25 * g0[2 * c + k, t] - value) + nb
                        parts[t] = parts[t] + m0[2 * c + k, t : t + 1, :] * inner
                for t in range(2):
                    r0[c, t] = parts[t]

            wait_near(r, False, True)
            unpack(r, unpack_v, (0,))
            loop(9, 23, sweep0, 7)
            loop(5, 11, residual0, 3)

            @pl.when(r > 0)
            def _():
                far_all(lambda dx, dy, i: g_copy(r - 1, dx, dy, i, False).wait_send())

            @pl.when(r == 0)
            def _():
                wait_near(CYCLES, True, False)
                unpack(CYCLES, unpack_g, (-1, 1))
                right_side((-1, 1))

            wait_near(r, False, False)
            unpack(r, unpack_v, (-1, 1))
            for low in (1, 23):
                loop(low, low + 8, sweep0, 8)
            for low in (1, 11):
                loop(low, low + 4, residual0, 4)

            def restrict0(c):
                for t in range(2):
                    f = r0[c, t, pl.ds(0, 16, stride=2), :] + r0[c, t, pl.ds(1, 16, stride=2), :]
                    g = f * (0.25 * w1[c, t : t + 1, :])
                    g1[c, t] = g
                    s1[c, t, 8:24, :] = g

            loop(1, 15, restrict0, 7)

            def residual1(c):
                parts = [0.0, 0.0]
                for k in range(2):
                    for t, (value, nb) in enumerate(around(s1, 2 * c + k, 16, 1)):
                        inner = (0.25 * c1) * value + nb
                        parts[t] = parts[t] + m1[2 * c + k, t : t + 1, :] * inner
                for t in range(2):
                    r1[c, t] = parts[t]

            loop(1, 7, residual1, 3)

            def restrict1(c):
                for t in range(2):
                    f = r1[c, t, pl.ds(0, 8, stride=2), :] + r1[c, t, pl.ds(1, 8, stride=2), :]
                    s2[c, t, 8:16, :] = f * (0.25 * w2[c, t : t + 1, :])

            for c in range(1, 7):
                restrict1(c)
            for k in range(4):
                own = s2[2 + k, 0, 8:16, :]
                gtx[r, 8 * k + 8 : 8 * k + 16, :] = own
                grx[r, REACH, 1, 8 * k + 8 : 8 * k + 16, :] = own
            for c in range(1, 3):
                part = 0.0
                for k in range(2):
                    ((value, nb),) = around(s2, 2 * c + k, 8, 2, halo=False)
                    inner = (0.25 * c2) * value + nb
                    part = part + m2[2 * c + k, 0:1, :] * inner
                r2[c - 1] = part
                f = r2[c - 1, pl.ds(0, 4, stride=2), :] + r2[c - 1, pl.ds(1, 4, stride=2), :]
                g = f * (0.25 * w3[c, 0:1, :])
                gtx[r, 4 * c - 4 : 4 * c, :] = g
                gtx[r, 36 + 4 * c : 40 + 4 * c, :] = g
                grx[r, REACH, 1, 4 * c - 4 : 4 * c, :] = g
            far_all(lambda dx, dy, i: g_copy(r, dx, dy, i, False).start())

            for i, (dx, dy) in enumerate(NEAR):
                when_there(dx, dy, lambda: near_copy(r, i, False, False).wait_send())

            @pl.when(r == 0)
            def _():
                profile_all(lambda dx, o: profile_copy(dx, o, False).wait_send())
                for i, (dx, dy) in enumerate(NEAR):
                    def leave():
                        block_copy("m", 0, dx, dy, i, len(NEAR), False).wait_send()
                        near_copy(CYCLES, i, False, True).wait_send()

                    when_there(dx, dy, leave)

            far_all(lambda dx, dy, i: g_copy(r, dx, dy, i, True).wait_recv())

            kx, kz, _ = coefficients(3)
            width = 2 * REACH + 1
            scale3 = []
            gs = []
            for d in range(width):
                there_x = jnp.logical_and(gx + d - REACH >= 0, gx + d - REACH < n_gx)
                valid = jnp.where(there_x, WEIGHT / c3, 0.0).astype(jnp.float32)
                scale3.append((valid, valid * halo_row))
                rows = slice(40, 48) if d == REACH - 1 else slice(0, 8)
                gs.append(
                    (
                        grx[r, d, 1, rows, :],
                        jnp.where(lane < 64, grx[r, d, 2, rows, :], grx[r, d, 0, rows, :]),
                    )
                )
            zero = jnp.zeros((8, 128), jnp.float32)
            vs = gs
            for sweep in range(SWEEPS):
                new = []
                for d in range(width):
                    mid, side = vs[d]
                    a, b = pltpu.roll(mid, 1, 1), pltpu.roll(side, 1, 1)
                    p, q = pltpu.roll(mid, 127, 1), pltpu.roll(side, 127, 1)
                    ys = (
                        jnp.where(lane == 0, b, a) + jnp.where(lane == 127, q, p),
                        jnp.where(lane == 0, a, b) + jnp.where(lane == 127, p, q),
                    )
                    pair = []
                    for t in range(2):
                        v = vs[d][t]
                        before = vs[d - 1][t] if d > 0 else zero
                        after = vs[d + 1][t] if d + 1 < width else zero
                        xs = pltpu.roll(v + jnp.where(sub >= 4, before, after), 4, 0)
                        zs = jnp.where(sub % 4 != 0, pltpu.roll(v, 1, 0), 0.0)
                        zs = zs + jnp.where(sub % 4 != 3, pltpu.roll(v, 7, 0), 0.0)
                        nb = kx * xs + ys[t] + kz * zs
                        pair.append(0.2 * v + scale3[d][t] * nb + gs[d][t])
                    new.append(tuple(pair))
                vs = new
            for c in range(4):
                d, k = REACH + (c + 1) // 2 - 1, (c + 1) % 2
                for t in range(2):
                    column = vs[d][t][4 * k : 4 * k + 4, :]
                    p3[c, t, pl.ds(0, 4, stride=2), :] = column
                    p3[c, t, pl.ds(1, 4, stride=2), :] = column

            def g2_of(c):
                d, k = (c - 2) // 4 + REACH, (c - 2) % 4
                rows = slice(8 * k + 8, 8 * k + 16)
                return (
                    grx[r, d, 1, rows, :],
                    jnp.where(lane < 64, grx[r, d, 2, rows, :], grx[r, d, 0, rows, :]),
                )

            for c in range(8):
                g = g2_of(c)
                for t in range(2):
                    s2[c, t, 8:16, :] = g[t] + p3[c // 2, t]
            for c in range(1, 7):
                valid = column_in(c, 4, 2)
                g = g2_of(c)
                for t, (value, nb) in enumerate(around(s2, c, 8, 2)):
                    new = 0.2 * value + weight_of(t, valid, 2) * nb + g[t]
                    p2[c, t, pl.ds(0, 8, stride=2), :] = new
                    p2[c, t, pl.ds(1, 8, stride=2), :] = new

            def correct1(c):
                for k in range(2):
                    for t in range(2):
                        s1[2 * c + k, t, 8:24, :] = g1[2 * c + k, t] + p2[c, t]

            loop(1, 7, correct1, 6)

            def post1(c):
                valid = column_in(c, 8, 4)
                for t, (value, nb) in enumerate(around(s1, c, 16, 1)):
                    new = 0.2 * value + weight_of(t, valid, 1) * nb + g1[c, t]
                    p1[c, t, pl.ds(0, 16, stride=2), :] = new
                    p1[c, t, pl.ds(1, 16, stride=2), :] = new

            loop(3, 13, post1, 5)

            def correct0(c):
                for k in range(2):
                    for t in range(2):
                        old = s0[2 * c + k, t, 8:40, :]
                        s0[2 * c + k, t, 8:40, :] = old + p1[c, t]

            loop(3, 13, correct0, 2)

            def post0(c):
                ((value, nb),) = around(s0, c, 32, 0, halo=False)
                v0[r + 1, c, 0, 8:40, :] = 0.2 * value + (WEIGHT / c0) * nb + g0[c, 0]

            loop(8, 16, post0, 8)

            @pl.when(r + 1 < CYCLES)
            def _():
                start_x(r + 1, False, (-1,))

            loop(16, 24, post0, 8)

            @pl.when(r + 1 < CYCLES)
            def _():
                start_x(r + 1, False, (1,))
                start_y(r + 1, lambda k: v0[r + 1, 8 + k, 0, 8:40, :], False)

            return carry

        lax.fori_loop(0, CYCLES, cycle, 0)

        for x in range(16):
            out[pl.ds(x, 32, stride=16), :] = v0[CYCLES, 8 + x, 0, 8:40, :]

        far_all(lambda dx, dy, i: g_copy(CYCLES - 1, dx, dy, i, False).wait_send())

    return kernel


def solution(mesh):
    n_gx, n_gy = mesh.shape["gx"], mesh.shape["gy"]
    f32 = jnp.float32
    near, far = len(NEAR), len(FAR)
    dma = pltpu.SemaphoreType.DMA
    vmem = pl.BlockSpec(memory_space=pltpu.VMEM)
    shapes = [
        (CYCLES + 1, 32, 2, 48, 128),
        (32, 2, 48, 128),
        (32, 2, 32, 128),
        (32, 2, 32, 128),
        (16, 2, 32, 128),
        (16, 2, 16, 128),
        (8, 2, 24, 128),
        (16, 2, 32, 128),
        (8, 2, 16, 128),
        (2, 8, 128),
        (16, 2, 32, 128),
        (8, 2, 16, 128),
        (4, 2, 8, 128),
        (32, 8, 128),
        (16, 8, 128),
        (8, 8, 128),
        (16, 8, 128),
        (8, 8, 128),
        (4, 8, 128),
        (32, 128),
        (3, 3, 32, 128),
        (32, 16),
        (3, n_gy, 32, 16),
        (CYCLES + 1, 32, 128),
        (CYCLES + 1, 3, 2, 32, 128),
        (CYCLES, 48, 128),
        (CYCLES, 2 * REACH + 1, 3, 48, 128),
        (512, 128),
        (512, 128),
    ]
    sems = [
        dma((CYCLES + 1, near)), dma((CYCLES + 1, near)), dma((near,)), dma((near,)),
        dma((CYCLES, far)), dma((CYCLES, far)), dma((3, n_gy)), dma((3, n_gy)), dma((2,)),
    ]
    call = pl.pallas_call(
        make_kernel(n_gx, n_gy),
        out_shape=jax.ShapeDtypeStruct((512, 128), f32),
        in_specs=[pl.BlockSpec(memory_space=pltpu.HBM)] * 2 + [vmem] * 3 + [pl.BlockSpec(memory_space=pltpu.SMEM)],
        out_specs=vmem,
        scratch_shapes=[pltpu.VMEM(shape, f32) for shape in shapes] + sems,
        compiler_params=pltpu.CompilerParams(
            collective_id=0, has_side_effects=True, vmem_limit_bytes=62 * 1024 * 1024
        ),
    )

    def per_device(source, first_guess, metric, terrain_slope, profile_rows, profile_map):
        result = call(
            source.reshape(512, 128), first_guess.reshape(512, 128),
            metric, terrain_slope, jnp.swapaxes(profile_rows, 1, 2), profile_map,
        )
        return result.reshape(source.shape)

    return jax.shard_map(
        per_device,
        mesh=mesh,
        in_specs=(
            P(None, None, "gx", "gy"),
            P(None, None, "gx", "gy"),
            P("gx", "gy"),
            P("gx", "gy"),
            P("gy", None, "gx"),
            P(),
        ),
        out_specs=P(None, None, "gx", "gy"),
        check_vma=False,
    )
```

```python
import jax
import jax.numpy as jnp
from jax import lax
from jax.experimental import pallas as pl
from jax.experimental.pallas import tpu as pltpu
from jax.sharding import PartitionSpec as P

CYCLES = 3
SWEEPS = 5
SIGMA = 0.05
WEIGHT = 0.8
REACH = 3
NEAR = tuple((dx, dy) for dx in (-1, 0, 1) for dy in (-1, 0, 1) if (dx, dy) != (0, 0))
FAR = tuple(
    (dx, dy) for dx in range(-REACH, REACH + 1) for dy in (-1, 0, 1) if (dx, dy) != (0, 0)
)
MESH = pl.DeviceIdType.MESH


def coefficients(grid_level):
    kx = 0.25**grid_level
    kz = 4.0 * kx
    return kx, kz, SIGMA + 2.0 * kx + 2.0 + 2.0 * kz


def loop(low, high, body, step=1):
    count = (high - low) // step

    def several(i, carry):
        for part in range(step):
            body(low + i * step + part)
        return carry

    lax.fori_loop(0, count, several, 0)
    for i in range(low + count * step, high):
        body(i)


def make_kernel(n_gx, n_gy):
    def kernel(
        source, guess, metric, slope, profile, table,
        out,
        v0, s0, f0, g0, s1, g1, s2, r0, r1, r2, p1, p2, p3,
        m0, m1, m2, w1, w2, w3, mtx, mrx, ptx, prx, ytx, yrx, gtx, grx,
        guess_here, source_here,
        near_send, near_recv, metric_send, metric_recv,
        g_send, g_recv, prof_send, prof_recv, local,
    ):
        gx, gy = lax.axis_index("gx"), lax.axis_index("gy")

        def there(dx, dy):
            x, y = gx + dx, gy + dy
            inside = jnp.logical_and(x >= 0, x < n_gx)
            return jnp.logical_and(inside, jnp.logical_and(y >= 0, y < n_gy))

        def device(dx, dy):
            return (gx + dx, gy + dy)

        lane = lax.broadcasted_iota(jnp.int32, (1, 128), 1)
        plus = jnp.where(gy + 1 < n_gy, 1.0, 0.0).astype(jnp.float32)
        minus = jnp.where(gy >= 1, 1.0, 0.0).astype(jnp.float32)
        halo_row = jnp.where(lane < 64, plus, minus)

        def column_in(c, per_device, first):
            position = gx * per_device + c - first
            return jnp.where(
                jnp.logical_and(position >= 0, position < n_gx * per_device), 1.0, 0.0
            ).astype(jnp.float32)

        guess_copy = pltpu.make_async_copy(guess, guess_here, local.at[0])
        source_copy = pltpu.make_async_copy(source, source_here, local.at[1])
        guess_copy.start()
        source_copy.start()

        barrier = pltpu.get_barrier_semaphore()
        total = jnp.int32(n_gy - 1)
        for o in range(1, n_gy):
            pl.semaphore_signal(
                barrier, inc=1, device_id=(gx, lax.rem(gy + o, n_gy)), device_id_type=MESH
            )
        for dx in (-1, 1):
            present = there(dx, 0)
            total = total + jnp.where(present, n_gy, 0)

            @pl.when(present)
            def _():
                for o in range(n_gy):
                    pl.semaphore_signal(
                        barrier, inc=1, device_id=(gx + dx, lax.rem(gy + o, n_gy)),
                        device_id_type=MESH,
                    )
        for dx, dy in FAR:
            if abs(dx) > 1:
                present = there(dx, dy)
                total = total + jnp.where(present, 1, 0)

                @pl.when(present)
                def _():
                    pl.semaphore_signal(
                        barrier, inc=1, device_id=device(dx, dy), device_id_type=MESH
                    )

        def clear(ref, columns, depth, lead=()):
            zero = jnp.zeros((8, 128), jnp.float32)

            def body(c):
                for t in range(2):
                    ref[(*lead, c, t, pl.ds(0, 8), slice(None))] = zero
                    ref[(*lead, c, t, pl.ds(8 + depth, 8), slice(None))] = zero

            loop(0, columns, body, 8)

        for i, (dx, dy) in enumerate(NEAR):
            @pl.when(jnp.logical_not(there(dx, dy)))
            def _():
                mrx[dx + 1, dy + 1] = jnp.ones((32, 128), jnp.float32)
                if dy != 0:
                    for r in range(CYCLES + 1):
                        yrx[r, dx + 1, (dy + 1) // 2] = jnp.zeros((32, 128), jnp.float32)
                else:
                    first = 0 if dx < 0 else 24

                    def body(c):
                        f0[first + c, 0] = jnp.zeros((32, 128), jnp.float32)
                        for r in range(CYCLES):
                            v0[r, first + c, 0, 8:40, :] = jnp.zeros((32, 128), jnp.float32)

                    loop(0, 8, body)
                    prx[dx + 1] = jnp.zeros((n_gy, 32, 16), jnp.float32)
        for dx, dy in FAR:
            @pl.when(jnp.logical_not(there(dx, dy)))
            def _():
                for r in range(CYCLES):
                    grx[r, dx + REACH, dy + 1] = jnp.zeros((48, 128), jnp.float32)

        ptx[...] = profile[0].T
        prx[1, gy] = ptx[...]
        mtx[0:16, :] = metric[...]
        mtx[16:32, :] = slope[...]
        mrx[1, 1] = mtx[...]
        guess_copy.wait()
        for x in range(16):
            v0[0, 8 + x, 0, 8:40, :] = guess_here[pl.ds(x, 32, stride=16), :]
        source_copy.wait()
        for x in range(16):
            f0[8 + x, 0] = source_here[pl.ds(x, 32, stride=16), :]
        pl.semaphore_wait(barrier, total)

        def profile_copy(dx, o, arriving):
            other = lax.rem(gy + (n_gy - o if arriving else o), n_gy)
            sx, sy = (dx, other) if arriving else (-dx, gy)
            return pltpu.make_async_remote_copy(
                src_ref=ptx, dst_ref=prx.at[sx + 1, sy],
                send_sem=prof_send.at[dx + 1, o], recv_sem=prof_recv.at[sx + 1, o],
                device_id=(gx + dx, other), device_id_type=MESH,
            )

        def profile_all(action):
            for dx in (-1, 0, 1):
                @pl.when(there(dx, 0))
                def _():
                    for o in range(1 if dx == 0 else 0, n_gy):
                        action(dx, o)

        def near_copy(r, i, arriving, is_g):
            dx, dy = NEAR[i]
            sx, sy = (dx, dy) if arriving else (-dx, -dy)
            slot = i if arriving else len(NEAR) - 1 - i
            if dy == 0:
                here = 8 if dx < 0 else 16
                land = 0 if sx < 0 else 24
                if is_g:
                    src = f0.at[pl.ds(here, 8), 0]
                    dst = f0.at[pl.ds(land, 8), 0]
                else:
                    src = v0.at[r, pl.ds(here, 8), 0, pl.ds(8, 32), :]
                    dst = v0.at[r, pl.ds(land, 8), 0, pl.ds(8, 32), :]
            else:
                src = ytx.at[r]
                dst = yrx.at[r, sx + 1, (sy + 1) // 2]
            return pltpu.make_async_remote_copy(
                src_ref=src, dst_ref=dst,
                send_sem=near_send.at[r, i], recv_sem=near_recv.at[r, slot],
                device_id=device(dx, dy), device_id_type=MESH,
            )

        def block_copy(kind, r, dx, dy, i, count, arriving):
            sx, sy = (dx, dy) if arriving else (-dx, -dy)
            slot = i if arriving else count - 1 - i
            if kind == "m":
                src, dst = mtx, mrx.at[sx + 1, sy + 1]
                ss, rs = metric_send.at[i], metric_recv.at[slot]
            else:
                step = -dx if arriving else dx
                rows = {-1: pl.ds(0, 24), 0: pl.ds(0, 40), 1: pl.ds(24, 24)}.get(
                    step, pl.ds(0, 8)
                )
                src, dst = gtx.at[r, rows], grx.at[r, sx + REACH, sy + 1, rows]
                ss, rs = g_send.at[r, i], g_recv.at[r, slot]
            return pltpu.make_async_remote_copy(
                src_ref=src, dst_ref=dst, send_sem=ss, recv_sem=rs,
                device_id=device(dx, dy), device_id_type=MESH,
            )

        def when_there(dx, dy, action):
            @pl.when(there(dx, dy))
            def _():
                action()

        def start_x(r, is_g, sides=(-1, 1)):
            for i, (dx, dy) in enumerate(NEAR):
                if dy == 0 and dx in sides:
                    when_there(dx, dy, lambda: near_copy(r, i, False, is_g).start())

        def start_y(r, load, is_g):
            packed = jnp.zeros((32, 128), jnp.float32)
            for k in range(16):
                turned = pltpu.roll(load(k), (8 * k + 4) % 128, 1)
                packed = jnp.where(lane // 8 == k, turned, packed)
            ytx[r] = packed
            for i, (dx, dy) in enumerate(NEAR):
                if dy != 0:
                    when_there(dx, dy, lambda: near_copy(r, i, False, is_g).start())

        def wait_near(r, is_g, direct=None):
            for i, (dx, dy) in enumerate(NEAR):
                if direct is not None and direct != (dx == 0):
                    continue
                when_there(dx, dy, lambda: near_copy(r, i, True, is_g).wait_recv())

        def unpack(r, store, parts=(-1, 0, 1)):
            for dx, first, k0, n in ((-1, 0, 8, 8), (0, 8, 0, 16), (1, 24, 0, 8)):
                if dx not in parts:
                    continue
                both = jnp.where(lane % 8 < 4, yrx[r, dx + 1, 0], yrx[r, dx + 1, 1])
                for j in range(n):
                    shift = (128 - (8 * (k0 + j) + 4)) % 128
                    store(first + j, pltpu.roll(both, shift, 1))

        profile_all(lambda dx, o: profile_copy(dx, o, False).start())
        for i, (dx, dy) in enumerate(NEAR):
            when_there(
                dx, dy, lambda: block_copy("m", 0, dx, dy, i, len(NEAR), False).start()
            )
        start_x(0, False)
        start_x(CYCLES, True)
        start_y(CYCLES, lambda k: f0[8 + k, 0], True)
        start_y(0, lambda k: v0[0, 8 + k, 0, 8:40, :], False)

        for r in range(CYCLES):
            clear(v0, 32, 32, (r,))
        clear(s0, 32, 32)
        clear(s1, 16, 16)
        clear(s2, 8, 8)

        for i, (dx, dy) in enumerate(NEAR):
            when_there(
                dx, dy, lambda: block_copy("m", 0, dx, dy, i, len(NEAR), True).wait_recv()
            )
        for c in range(32):
            dx, k = (c - 8) // 16, (c - 8) % 16
            m0[c, 0:1, :] = mrx[dx + 1, 1, k : k + 1, :]
            m0[c, 1:2, :] = jnp.where(
                lane < 64, mrx[dx + 1, 2, k : k + 1, :], mrx[dx + 1, 0, k : k + 1, :]
            )
        for fine, coarse, weights, level, first, span, low, high in (
            (m0, m1, w1, 1, 4, 8, 1, 15),
            (m1, m2, w2, 2, 2, 4, 1, 7),
            (m2, None, w3, 3, 1, 2, 1, 3),
        ):
            centre = coefficients(level)[2]
            for c in range(low, high):
                for t in range(2):
                    row = 0.5 * (
                        fine[2 * c, t : t + 1, :] + fine[2 * c + 1, t : t + 1, :]
                    )
                    if coarse is not None:
                        coarse[c, t : t + 1, :] = row
                    valid = column_in(c, span, first)
                    if t == 1:
                        valid = valid * halo_row
                    weights[c, t : t + 1, :] = valid * (WEIGHT / (row * centre))

        def around(ref, c, depth, grid_level, lead=(), halo=True):
            kx, kz, _ = coefficients(grid_level)

            def at(column, t, shift=0):
                return ref[(*lead, column, t, pl.ds(8 + shift, depth), slice(None))]

            mid, side = at(c, 0), at(c, 1)
            a, b = pltpu.roll(mid, 1, 1), pltpu.roll(side, 1, 1)
            p, q = pltpu.roll(mid, 127, 1), pltpu.roll(side, 127, 1)
            ys = (
                jnp.where(lane == 0, b, a) + jnp.where(lane == 127, q, p),
                jnp.where(lane == 0, a, b) + jnp.where(lane == 127, p, q) if halo else None,
            )
            result = []
            for t in range(2 if halo else 1):
                total = kx * (at(c - 1, t) + at(c + 1, t)) + ys[t]
                total = total + kz * (at(c, t, -1) + at(c, t, 1))
                result.append(((mid, side)[t], total))
            return result

        def weight_of(t, valid, grid_level):
            scale = (WEIGHT / coefficients(grid_level)[2]) * valid
            return scale if t == 0 else scale * halo_row

        def unpack_g(c, value):
            f0[c, 1] = value

        centre0 = coefficients(0)[2]

        def right_side(parts):
            for dx, first, k0, n in ((-1, 0, 8, 8), (0, 8, 0, 16), (1, 24, 0, 8)):
                if dx not in parts:
                    continue
                own, above, below = (
                    prx[dx + 1, strip]
                    for strip in (
                        table[gy],
                        table[jnp.minimum(gy + 1, n_gy - 1)],
                        table[jnp.maximum(gy - 1, 0)],
                    )
                )
                for j in range(n):
                    c, k = first + j, k0 + j
                    column = slice(k, k + 1)
                    row = 16 + k
                    valid = column_in(c, 16, 8) * (WEIGHT / centre0)
                    g0[c, 0] = (f0[c, 0] + own[:, column] * mrx[dx + 1, 1, row : row + 1, :]) * (
                        valid / m0[c, 0:1, :]
                    )
                    side = jnp.where(lane < 64, above[:, column], below[:, column])
                    steep = jnp.where(
                        lane < 64, mrx[dx + 1, 2, row : row + 1, :], mrx[dx + 1, 0, row : row + 1, :]
                    )
                    g0[c, 1] = (f0[c, 1] + side * steep) * (valid * halo_row / m0[c, 1:2, :])

        profile_all(lambda dx, o: profile_copy(dx, o, True).wait_recv())
        wait_near(CYCLES, True, True)
        unpack(CYCLES, unpack_g, (0,))
        right_side((0,))

        def g_copy(r, dx, dy, i, arriving):
            return block_copy("g", r, dx, dy, i, len(FAR), arriving)

        def far_all(action):
            for i, (dx, dy) in enumerate(FAR):
                when_there(dx, dy, lambda: action(dx, dy, i))

        sub = lax.broadcasted_iota(jnp.int32, (8, 128), 0)

        def cycle(r, carry):
            c0, c1, c2, c3 = (coefficients(level)[2] for level in range(4))
            def unpack_v(c, value):
                v0[r, c, 1, 8:40, :] = value

            def sweep0(c):
                valid = column_in(c, 16, 8)
                for t, (value, nb) in enumerate(around(v0, c, 32, 0, (r,))):
                    s0[c, t, 8:40, :] = 0.2 * value + weight_of(t, valid, 0) * nb + g0[c, t]

            def residual0(c):
                parts = [0.0, 0.0]
                for k in range(2):
                    for t, (value, nb) in enumerate(around(s0, 2 * c + k, 32, 0)):
                        inner = c0 * (1.25 * g0[2 * c + k, t] - value) + nb
                        parts[t] = parts[t] + m0[2 * c + k, t : t + 1, :] * inner
                for t in range(2):
                    r0[c, t] = parts[t]

            wait_near(r, False, True)
            unpack(r, unpack_v, (0,))
            loop(9, 23, sweep0, 14)
            loop(5, 11, residual0, 6)

            @pl.when(r > 0)
            def _():
                far_all(lambda dx, dy, i: g_copy(r - 1, dx, dy, i, False).wait_send())

            @pl.when(r == 0)
            def _():
                wait_near(CYCLES, True, False)
                unpack(CYCLES, unpack_g, (-1, 1))
                right_side((-1, 1))

            wait_near(r, False, False)
            unpack(r, unpack_v, (-1, 1))
            for low in (1, 23):
                loop(low, low + 8, sweep0, 8)
            for low in (1, 11):
                loop(low, low + 4, residual0, 4)

            def restrict0(c):
                for t in range(2):
                    f = r0[c, t, pl.ds(0, 16, stride=2), :] + r0[c, t, pl.ds(1, 16, stride=2), :]
                    g = f * (0.25 * w1[c, t : t + 1, :])
                    g1[c, t] = g
                    s1[c, t, 8:24, :] = g

            loop(1, 15, restrict0, 14)

            def residual1(c):
                parts = [0.0, 0.0]
                for k in range(2):
                    for t, (value, nb) in enumerate(around(s1, 2 * c + k, 16, 1)):
                        inner = (0.25 * c1) * value + nb
                        parts[t] = parts[t] + m1[2 * c + k, t : t + 1, :] * inner
                for t in range(2):
                    r1[c, t] = parts[t]

            loop(1, 7, residual1, 6)

            def restrict1(c):
                for t in range(2):
                    f = r1[c, t, pl.ds(0, 8, stride=2), :] + r1[c, t, pl.ds(1, 8, stride=2), :]
                    s2[c, t, 8:16, :] = f * (0.25 * w2[c, t : t + 1, :])

            for c in range(1, 7):
                restrict1(c)
            for k in range(4):
                own = s2[2 + k, 0, 8:16, :]
                gtx[r, 8 * k + 8 : 8 * k + 16, :] = own
                grx[r, REACH, 1, 8 * k + 8 : 8 * k + 16, :] = own
            for c in range(1, 3):
                part = 0.0
                for k in range(2):
                    ((value, nb),) = around(s2, 2 * c + k, 8, 2, halo=False)
                    inner = (0.25 * c2) * value + nb
                    part = part + m2[2 * c + k, 0:1, :] * inner
                r2[c - 1] = part
                f = r2[c - 1, pl.ds(0, 4, stride=2), :] + r2[c - 1, pl.ds(1, 4, stride=2), :]
                g = f * (0.25 * w3[c, 0:1, :])
                gtx[r, 4 * c - 4 : 4 * c, :] = g
                gtx[r, 36 + 4 * c : 40 + 4 * c, :] = g
                grx[r, REACH, 1, 4 * c - 4 : 4 * c, :] = g
            far_all(lambda dx, dy, i: g_copy(r, dx, dy, i, False).start())

            for i, (dx, dy) in enumerate(NEAR):
                when_there(dx, dy, lambda: near_copy(r, i, False, False).wait_send())

            @pl.when(r == 0)
            def _():
                profile_all(lambda dx, o: profile_copy(dx, o, False).wait_send())
                for i, (dx, dy) in enumerate(NEAR):
                    def leave():
                        block_copy("m", 0, dx, dy, i, len(NEAR), False).wait_send()
                        near_copy(CYCLES, i, False, True).wait_send()

                    when_there(dx, dy, leave)

            far_all(lambda dx, dy, i: g_copy(r, dx, dy, i, True).wait_recv())

            kx, kz, _ = coefficients(3)
            width = 2 * REACH + 1
            scale3 = []
            gs = []
            for d in range(width):
                there_x = jnp.logical_and(gx + d - REACH >= 0, gx + d - REACH < n_gx)
                valid = jnp.where(there_x, WEIGHT / c3, 0.0).astype(jnp.float32)
                scale3.append((valid, valid * halo_row))
                rows = slice(40, 48) if d == REACH - 1 else slice(0, 8)
                gs.append(
                    (
                        grx[r, d, 1, rows, :],
                        jnp.where(lane < 64, grx[r, d, 2, rows, :], grx[r, d, 0, rows, :]),
                    )
                )
            zero = jnp.zeros((8, 128), jnp.float32)
            vs = gs
            for sweep in range(SWEEPS):
                new = []
                for d in range(width):
                    mid, side = vs[d]
                    a, b = pltpu.roll(mid, 1, 1), pltpu.roll(side, 1, 1)
                    p, q = pltpu.roll(mid, 127, 1), pltpu.roll(side, 127, 1)
                    ys = (
                        jnp.where(lane == 0, b, a) + jnp.where(lane == 127, q, p),
                        jnp.where(lane == 0, a, b) + jnp.where(lane == 127, p, q),
                    )
                    pair = []
                    for t in range(2):
                        v = vs[d][t]
                        before = vs[d - 1][t] if d > 0 else zero
                        after = vs[d + 1][t] if d + 1 < width else zero
                        xs = pltpu.roll(v + jnp.where(sub >= 4, before, after), 4, 0)
                        zs = jnp.where(sub % 4 != 0, pltpu.roll(v, 1, 0), 0.0)
                        zs = zs + jnp.where(sub % 4 != 3, pltpu.roll(v, 7, 0), 0.0)
                        nb = kx * xs + ys[t] + kz * zs
                        pair.append(0.2 * v + scale3[d][t] * nb + gs[d][t])
                    new.append(tuple(pair))
                vs = new
            for c in range(4):
                d, k = REACH + (c + 1) // 2 - 1, (c + 1) % 2
                for t in range(2):
                    column = vs[d][t][4 * k : 4 * k + 4, :]
                    p3[c, t, pl.ds(0, 4, stride=2), :] = column
                    p3[c, t, pl.ds(1, 4, stride=2), :] = column

            def g2_of(c):
                d, k = (c - 2) // 4 + REACH, (c - 2) % 4
                rows = slice(8 * k + 8, 8 * k + 16)
                return (
                    grx[r, d, 1, rows, :],
                    jnp.where(lane < 64, grx[r, d, 2, rows, :], grx[r, d, 0, rows, :]),
                )

            for c in range(8):
                g = g2_of(c)
                for t in range(2):
                    s2[c, t, 8:16, :] = g[t] + p3[c // 2, t]
            for c in range(1, 7):
                valid = column_in(c, 4, 2)
                g = g2_of(c)
                for t, (value, nb) in enumerate(around(s2, c, 8, 2)):
                    new = 0.2 * value + weight_of(t, valid, 2) * nb + g[t]
                    p2[c, t, pl.ds(0, 8, stride=2), :] = new
                    p2[c, t, pl.ds(1, 8, stride=2), :] = new

            def correct1(c):
                for k in range(2):
                    for t in range(2):
                        s1[2 * c + k, t, 8:24, :] = g1[2 * c + k, t] + p2[c, t]

            loop(1, 7, correct1, 6)

            def post1(c):
                valid = column_in(c, 8, 4)
                for t, (value, nb) in enumerate(around(s1, c, 16, 1)):
                    new = 0.2 * value + weight_of(t, valid, 1) * nb + g1[c, t]
                    p1[c, t, pl.ds(0, 16, stride=2), :] = new
                    p1[c, t, pl.ds(1, 16, stride=2), :] = new

            loop(3, 13, post1, 10)

            def correct0(c):
                for k in range(2):
                    for t in range(2):
                        old = s0[2 * c + k, t, 8:40, :]
                        s0[2 * c + k, t, 8:40, :] = old + p1[c, t]

            loop(3, 13, correct0, 2)

            def post0(c):
                ((value, nb),) = around(s0, c, 32, 0, halo=False)
                v0[r + 1, c, 0, 8:40, :] = 0.2 * value + (WEIGHT / c0) * nb + g0[c, 0]

            loop(8, 16, post0, 8)

            @pl.when(r + 1 < CYCLES)
            def _():
                start_x(r + 1, False, (-1,))

            loop(16, 24, post0, 8)

            @pl.when(r + 1 < CYCLES)
            def _():
                start_x(r + 1, False, (1,))
                start_y(r + 1, lambda k: v0[r + 1, 8 + k, 0, 8:40, :], False)

            return carry

        lax.fori_loop(0, CYCLES, cycle, 0)

        for x in range(16):
            out[pl.ds(x, 32, stride=16), :] = v0[CYCLES, 8 + x, 0, 8:40, :]

        far_all(lambda dx, dy, i: g_copy(CYCLES - 1, dx, dy, i, False).wait_send())

    return kernel


def solution(mesh):
    n_gx, n_gy = mesh.shape["gx"], mesh.shape["gy"]
    f32 = jnp.float32
    near, far = len(NEAR), len(FAR)
    dma = pltpu.SemaphoreType.DMA
    vmem = pl.BlockSpec(memory_space=pltpu.VMEM)
    shapes = [
        (CYCLES + 1, 32, 2, 48, 128),
        (32, 2, 48, 128),
        (32, 2, 32, 128),
        (32, 2, 32, 128),
        (16, 2, 32, 128),
        (16, 2, 16, 128),
        (8, 2, 24, 128),
        (16, 2, 32, 128),
        (8, 2, 16, 128),
        (2, 8, 128),
        (16, 2, 32, 128),
        (8, 2, 16, 128),
        (4, 2, 8, 128),
        (32, 8, 128),
        (16, 8, 128),
        (8, 8, 128),
        (16, 8, 128),
        (8, 8, 128),
        (4, 8, 128),
        (32, 128),
        (3, 3, 32, 128),
        (32, 16),
        (3, n_gy, 32, 16),
        (CYCLES + 1, 32, 128),
        (CYCLES + 1, 3, 2, 32, 128),
        (CYCLES, 48, 128),
        (CYCLES, 2 * REACH + 1, 3, 48, 128),
        (512, 128),
        (512, 128),
    ]
    sems = [
        dma((CYCLES + 1, near)), dma((CYCLES + 1, near)), dma((near,)), dma((near,)),
        dma((CYCLES, far)), dma((CYCLES, far)), dma((3, n_gy)), dma((3, n_gy)), dma((2,)),
    ]
    call = pl.pallas_call(
        make_kernel(n_gx, n_gy),
        out_shape=jax.ShapeDtypeStruct((512, 128), f32),
        in_specs=[pl.BlockSpec(memory_space=pltpu.HBM)] * 2 + [vmem] * 3 + [pl.BlockSpec(memory_space=pltpu.SMEM)],
        out_specs=vmem,
        scratch_shapes=[pltpu.VMEM(shape, f32) for shape in shapes] + sems,
        compiler_params=pltpu.CompilerParams(
            collective_id=0, has_side_effects=True, vmem_limit_bytes=62 * 1024 * 1024
        ),
    )

    def per_device(source, first_guess, metric, terrain_slope, profile_rows, profile_map):
        result = call(
            source.reshape(512, 128), first_guess.reshape(512, 128),
            metric, terrain_slope, jnp.swapaxes(profile_rows, 1, 2), profile_map,
        )
        return result.reshape(source.shape)

    return jax.shard_map(
        per_device,
        mesh=mesh,
        in_specs=(
            P(None, None, "gx", "gy"),
            P(None, None, "gx", "gy"),
            P("gx", "gy"),
            P("gx", "gy"),
            P("gy", None, "gx"),
            P(),
        ),
        out_specs=P(None, None, "gx", "gy"),
        check_vma=False,
    )
```
